512 devices in a mesh: section: 8 (over z_hi, x), tensor: 64 (over y, z_lo, core).
Axes of the slice: x: 4, y: 8, z: 8 (z_hi: 2, z_lo: 4; z = z_hi * 4 + z_lo), core: 2. Of those that a mesh axis runs over, the one named last changes fastest.
Arguments:
- activations: bfloat16 [8, 1024, 8192], P('section', None, 'tensor'), may hold values from -6 to 6
- conv_weight: bfloat16 [8, 4, 8192], P('section', None, 'tensor'), may hold values from -3 to 3
- step_size: float32 [8, 1024, 128], P('section', None, 'tensor'), may hold values from 0.01 to 0.1
- decay_rate: float32 [8, 128], P('section', 'tensor'), may hold values from 0.005 to 1
- skip_gain: float32 [8, 128], P('section', 'tensor'), may hold values from 0.5 to 1.5
- b_matrix: bfloat16 [8, 4, 256, 2048], P('section', None, 'tensor'), may hold values from -0.375 to 0.375
- c_matrix: bfloat16 [8, 4, 256, 2048], P('section', None, 'tensor'), may hold values from -6 to 6
- top_grad: bfloat16 [4, 256, 8192], P(None, 'tensor'), may hold values from -6 to 6
Outputs:
- stream_grad: bfloat16 [8, 4, 256, 8192], P('section', None, 'tensor')
- conv_grad: float32 [8, 4, 8192], P('section', None, 'tensor')
The draws below stay inside these ranges and needn't reach their ends.
All inputs are finite; a program needn't handle non-finite values.
Results may differ from the reference program's by a relative error of at most 0.035.
Values may be sent and summed in bfloat16 or wider, within the bound.
A program may use at most 128 MiB of HBM per device.

```python
import math
import jax
import jax.numpy as jnp
from jax import lax

H = 128
P_SIZE = 64
N = 256
G = 8
K = 4
BLOCKS = 4
CL = 256
SEQ = 1024
LAYERS = 8
N_SECTION = 8


def shard_levels(key, shape, split, smallest, largest):
    gain, own = 1.0, jax.random.fold_in(key, 6)
    for axis_at, parts in split:
        steps = jnp.exp(jax.random.uniform(jax.random.fold_in(own, axis_at), (parts,), jnp.float32, smallest / len(split), largest / len(split)))
        gain = gain * jnp.repeat(steps, shape[axis_at] // parts).reshape([-1 if axis == axis_at else 1 for axis in range(len(shape))])
    return gain


def normal_values(key, extent, spread, reach, cuts=(), held_as=jnp.bfloat16):
    loudness = shard_levels(key, extent, cuts, -0.22, 0.18) if cuts else 1.0
    values = jax.random.normal(key, extent, jnp.float32) * spread * loudness
    return jnp.minimum(jnp.maximum(values, -reach), reach).astype(held_as)


def setup_inputs(seed: int = 0) -> dict:
    keys = jax.random.split(jax.random.key(seed), 9)
    return {
        "activations": normal_values(keys[0], (LAYERS, SEQ, H * P_SIZE), 1.0, 6.0, ((0, 8), (2, 64))),
        "conv_weight": normal_values(keys[1], (LAYERS, K, H * P_SIZE), K ** -0.5, 3.0, ((0, 8), (2, 64))),
        "step_size": jnp.clip(jnp.exp(math.log(0.1) - 2.3025851 * jax.random.uniform(keys[2], (LAYERS, SEQ, H), jnp.float32) ** shard_levels(keys[2], (LAYERS, SEQ, H), ((0, 8), (2, 64)), -0.2, 0.2)), 0.01, 0.1),
        "decay_rate": jnp.clip(jnp.exp(math.log(1.0) - 5.2983174 * jax.random.uniform(keys[3], (LAYERS, H), jnp.float32) ** shard_levels(keys[3], (LAYERS, H), ((0, 8), (1, 64)), -0.2, 0.2)), 0.005, 1.0),
        "skip_gain": jnp.clip(1.0 + 0.1 * jax.random.normal(keys[4], (LAYERS, H), jnp.float32), 0.5, 1.5),
        "b_matrix": normal_values(keys[5], (LAYERS, BLOCKS, CL, G * N), N ** -0.5, 0.375, ((0, 8), (2, 64))),
        "c_matrix": normal_values(keys[6], (LAYERS, BLOCKS, CL, G * N), 1.0, 6.0, ((0, 8), (2, 64))),
        "top_grad": normal_values(keys[7], (BLOCKS, CL, H * P_SIZE), 1.0, 6.0, ((1, 64),)),
    }


def reference(activations, conv_weight, step_size, decay_rate, skip_gain, b_matrix, c_matrix, top_grad):
    length = BLOCKS * CL
    hidden = H * P_SIZE
    per_group = H // G
    causal = jnp.arange(CL)[:, None] >= jnp.arange(CL)[None, :]
    upstream = top_grad.reshape(length, hidden)
    grad_list = [None] * N_SECTION
    conv_list = [None] * N_SECTION
    for depth in range(N_SECTION - 1, -1, -1):
        inputs = activations[depth].astype(jnp.float32)
        weights = conv_weight[depth].astype(jnp.float32)
        padded = jnp.concatenate([jnp.zeros((K - 1, hidden), jnp.float32), inputs], axis=0)
        preact = jnp.zeros((length, hidden), jnp.float32)
        for tap_index in range(K):
            preact = preact + weights[tap_index] * padded[K - 1 - tap_index:K - 1 - tap_index + length]
        logistic = jax.nn.sigmoid(preact)
        slope = logistic * (1.0 + preact * (1.0 - logistic))
        step_rows = step_size[depth].reshape(BLOCKS, CL, H)
        decay_all = jnp.cumsum(-step_rows * decay_rate[depth][None, None, :], axis=1)
        b_rows = b_matrix[depth].reshape(BLOCKS, CL, G, N)
        c_rows = c_matrix[depth].reshape(BLOCKS, CL, G, N)
        grad_all = upstream.reshape(BLOCKS, CL, H, P_SIZE)
        carried = jnp.zeros((H, N, P_SIZE), jnp.float32)
        window_rows = jnp.zeros((K - 1, hidden), jnp.float32)
        conv_sum = jnp.zeros((K, hidden), jnp.float32)
        pieces = [None] * BLOCKS
        for block_at in range(BLOCKS - 1, -1, -1):
            decay_sum = decay_all[block_at]
            decay_end = decay_sum[-1]
            step_block = step_rows[block_at]
            b_block = b_rows[block_at].astype(jnp.float32)
            c_block = c_rows[block_at].astype(jnp.float32)
            scores = jnp.einsum("jgn,ign->gji", c_block, b_block)
            scores = jnp.repeat(scores, per_group, axis=0)
            decay_t = decay_sum.T
            decay_gap = decay_t[:, :, None] - decay_t[:, None, :]
            factor = jnp.exp(jnp.where(causal[None], decay_gap, 0.0))
            weight = jnp.where(causal[None], factor * scores * step_block.T[:, None, :], 0.0).astype(jnp.bfloat16)
            weight = lax.optimization_barrier(weight).astype(jnp.float32)
            grad_heads = grad_all[block_at].astype(jnp.float32)
            inside = jnp.einsum("hji,jhp->ihp", weight, grad_heads)
            carried_b = lax.optimization_barrier(carried.astype(jnp.bfloat16)).astype(jnp.float32)
            through = jnp.einsum("ign,gqnp->igqp", b_block, carried_b.reshape(G, per_group, N, P_SIZE)).reshape(CL, H, P_SIZE)
            factor_in = step_block * jnp.exp(decay_end[None, :] - decay_sum)
            grad_mix = inside + factor_in[:, :, None] * through + skip_gain[depth][None, :, None] * grad_heads
            c_heads = jnp.repeat(c_block, per_group, axis=1)
            scaled = (jnp.exp(decay_sum)[:, :, None] * c_heads).astype(jnp.bfloat16)
            scaled = lax.optimization_barrier(scaled).astype(jnp.float32)
            carried = jnp.exp(decay_end)[:, None, None] * carried + jnp.einsum("ihn,ihp->hnp", scaled, grad_heads)
            grad_pre = grad_mix.reshape(CL, hidden) * slope[block_at * CL:(block_at + 1) * CL]
            extended = jnp.concatenate([grad_pre, window_rows], axis=0)
            grad_in = jnp.zeros((CL, hidden), jnp.float32)
            for tap_index in range(K):
                grad_in = grad_in + weights[tap_index] * extended[tap_index:tap_index + CL]
                start_row = block_at * CL + K - 1 - tap_index
                conv_sum = conv_sum.at[tap_index].add(jnp.sum(grad_pre * padded[start_row:start_row + CL], axis=0))
            window_rows = grad_pre[:K - 1]
            grad_back = lax.optimization_barrier(grad_in.astype(jnp.bfloat16)).astype(jnp.float32)
            pieces[block_at] = (upstream[block_at * CL:(block_at + 1) * CL].astype(jnp.float32) + grad_back).astype(jnp.bfloat16)
        stream = jnp.concatenate(pieces, axis=0)
        grad_list[depth] = stream.reshape(BLOCKS, CL, hidden)
        conv_list[depth] = conv_sum
        upstream = stream
    return jnp.stack(grad_list), jnp.stack(conv_list)
```

```python
import functools

import jax
import jax.numpy as jnp
from jax import lax
from jax.experimental import pallas as pl
from jax.experimental.pallas import tpu as pltpu
from jax.sharding import PartitionSpec as P

P_SIZE = 64
N = 256
K = 4
BLOCKS = 4
CHUNK = 128
PAD = 8
F32 = jnp.float32
BF16 = jnp.bfloat16


def dot(a, b):
    return jnp.dot(a, b, preferred_element_type=F32)


def kernel(
    sizes,
    act_ref,
    taps_ref,
    step_ref,
    rate_ref,
    skip_ref,
    b_ref,
    c_ref,
    top_ref,
    out_ref,
    conv_ref,
    staged,
    bc_send,
    bc_rows,
    bc_all,
    top_send,
    top_rows,
    top_all,
    act_pad,
    slope,
    grow,
    shrink,
    b_flat,
    c_flat,
    scores,
    carried,
    dy,
    stream,
    extended,
    out_send,
    out_rows,
    out_all,
    bc1_s,
    bc1_r,
    bc2_s,
    bc2_r,
    bc3_s,
    bc3_r,
    top1_s,
    top1_r,
    top2_s,
    top2_r,
    hop_s,
    hop_r,
    out1_s,
    out1_r,
    out2_s,
    out2_r,
    local_s,
):
    sections, ys, ws, chunk = sizes
    block = 4 * ys * ws
    length = BLOCKS * block
    chunks = length // chunk
    zs = ws // 2
    run = 4 * ws
    sec = lax.axis_index("section")
    pos = lax.axis_index("tensor")
    y = pos // ws
    w = pos % ws
    z = w // 2
    core = w % 2
    top_layer = sec == sections - 1

    def remote(src, dst, send, recv, section, tensor):
        return pltpu.make_async_remote_copy(
            src_ref=src,
            dst_ref=dst,
            send_sem=send,
            recv_sem=recv,
            device_id=(section, tensor),
            device_id_type=pl.DeviceIdType.MESH,
        )

    def other_y(d):
        return lax.rem(y + d, ys) * ws + w

    def other_w(d):
        return y * ws + lax.rem(w + d, ws)

    def other_z(d):
        return y * ws + lax.rem(z + d, zs) * 2 + core

    sibling = y * ws + z * 2 + (1 - core)

    barrier = pltpu.get_barrier_semaphore()

    def greet(section, tensor):
        pl.semaphore_signal(
            barrier, inc=1, device_id=(section, tensor), device_id_type=pl.DeviceIdType.MESH
        )

    for d in range(1, ys):
        greet(sec, other_y(d))
    for d in range(1, ws):
        greet(sec, other_w(d))

    greet(lax.rem(sec + sections - 1, sections), pos)
    greet(lax.rem(sec + 1, sections), pos)

    for at in range(BLOCKS):
        staged[4 * at : 4 * at + 4, 0 : ys * N] = b_ref[at].astype(F32)
        staged[4 * at : 4 * at + 4, ys * N : 2 * ys * N] = c_ref[at].astype(F32)
    for g in range(ys):
        bc_send[g, :, 0:N] = staged[:, g * N : (g + 1) * N].astype(BF16)
        bc_send[g, :, N : 2 * N] = staged[:, (ys + g) * N : (ys + g + 1) * N].astype(BF16)

    pl.semaphore_wait(barrier, ys + ws)

    def bc1(d):
        return remote(
            bc_send.at[lax.rem(y + d, ys)], bc_rows.at[y], bc1_s.at[d], bc1_r.at[d], sec, other_y(d)
        )

    def bc1_in(d):
        at = lax.rem(y + ys - d, ys)
        return remote(bc_send.at[at], bc_rows.at[at], bc1_s.at[d], bc1_r.at[d], sec, other_y(d))

    for d in range(1, ys):
        bc1(d).start()
    bc_rows[pl.ds(y, 1)] = bc_send[pl.ds(y, 1)]

    def top1(d):
        return remote(
            top_send.at[lax.rem(y + d, ys)],
            top_rows.at[y],
            top1_s.at[d],
            top1_r.at[d],
            sec,
            other_y(d),
        )

    def top1_in(d):
        at = lax.rem(y + ys - d, ys)
        return remote(top_send.at[at], top_rows.at[at], top1_s.at[d], top1_r.at[d], sec, other_y(d))

    wide = ws * 2 * P_SIZE

    @pl.when(top_layer)
    def _():
        for at in range(BLOCKS):
            staged[4 * at : 4 * at + 4, :] = top_ref[at].astype(F32)
        for g in range(ys):
            top_send[g] = staged[:, g * wide : (g + 1) * wide].astype(BF16)
        for d in range(1, ys):
            top1(d).start()
        top_rows[pl.ds(y, 1)] = top_send[pl.ds(y, 1)]

    act_pad[0:PAD, :] = jnp.zeros((PAD, 2 * P_SIZE), F32)
    act_pad[PAD:, :] = act_ref[...].astype(F32)
    taps = taps_ref[...].astype(F32)
    first = lax.broadcasted_iota(jnp.int32, (1, 2 * P_SIZE), 1) < P_SIZE
    rate = jnp.where(first, rate_ref[:, 0:1], rate_ref[:, 1:2])
    skip = jnp.where(first, skip_ref[:, 0:1], skip_ref[:, 1:2])
    row_at = lax.broadcasted_iota(jnp.int32, (chunk, chunk), 0)
    col_at = lax.broadcasted_iota(jnp.int32, (chunk, chunk), 1)
    lower = (row_at >= col_at).astype(F32).astype(BF16)
    for at in range(chunks):
        rows = slice(at * chunk, (at + 1) * chunk)
        preact = jnp.zeros((chunk, 2 * P_SIZE), F32)
        for k in range(K):
            start = PAD + at * chunk - k
            preact = preact + taps[k : k + 1] * act_pad[start : start + chunk, :]
        logistic = 1.0 / (1.0 + jnp.exp(-preact))
        slope[rows, :] = logistic * (1.0 + preact * (1.0 - logistic))
        step = jnp.concatenate(
            [jnp.broadcast_to(step_ref[h : h + 1, rows], (P_SIZE, chunk)) for h in range(2)], axis=0
        ).T
        high = step.astype(BF16)
        rest = step - high.astype(F32)
        mid = rest.astype(BF16)
        low = (rest - mid.astype(F32)).astype(BF16)
        decay = -rate * (dot(lower, high) + dot(lower, mid) + dot(lower, low))
        grow[rows, :] = jnp.exp(decay)
        shrink[rows, :] = step * jnp.exp(-decay)
    carried[...] = jnp.zeros_like(carried)
    extended[length:, :] = jnp.zeros((PAD, 2 * P_SIZE), F32)

    side = 16 * ws
    out_at = lax.broadcasted_iota(jnp.int32, (side, side), 0)
    in_at = lax.broadcasted_iota(jnp.int32, (side, side), 1)

    def source_of(at):
        return ((at // 4) % ws) * 16 + (at // run) * 4 + at % 4

    gather = (source_of(out_at) == in_at).astype(F32).astype(BF16)
    scatter = (source_of(in_at) == out_at).astype(F32).astype(BF16)

    def part(of):
        return bc_all.at[:, pl.ds(pl.multiple_of(of * 16, 16), 16), :]

    def bc2(d):
        to = sibling if d == 0 else other_z(d)
        return remote(bc_rows, part(w), bc2_s.at[d], bc2_r.at[d], sec, to)

    def bc2_in(d):
        of = z * 2 + (1 - core) if d == 0 else lax.rem(z + zs - d, zs) * 2 + core
        return remote(bc_rows, part(of), bc2_s.at[d], bc2_r.at[d], sec, sibling)

    def bc3(d):
        of = lax.rem(z + zs - d, zs) * 2 + core
        return remote(part(of), part(of), bc3_s.at[d], bc3_r.at[d], sec, sibling)

    def bc3_in(d):
        of = lax.rem(z + zs - d, zs) * 2 + (1 - core)
        return remote(part(of), part(of), bc3_s.at[d], bc3_r.at[d], sec, sibling)

    for d in range(1, ys):
        bc1_in(d).wait_recv()
    for d in list(range(zs - 1, 0, -1)) + [0]:
        bc2(d).start()
    own = pltpu.make_async_copy(bc_rows, part(w), local_s.at[0])
    own.start()

    def columns(of):
        return pl.ds(pl.multiple_of(of * 2 * P_SIZE, 2 * P_SIZE), 2 * P_SIZE)

    def slab(of):
        return pl.ds(pl.multiple_of(of * 16, 16), 16)

    def top2(d):
        to = lax.rem(w + d, ws)
        return remote(
            top_rows.at[:, :, columns(to)],
            top_all.at[:, slab(w), :],
            top2_s.at[d],
            top2_r.at[d],
            sec,
            other_w(d),
        )

    def top2_in(d):
        of = lax.rem(w + ws - d, ws)
        return remote(
            top_rows.at[:, :, columns(of)],
            top_all.at[:, slab(of), :],
            top2_s.at[d],
            top2_r.at[d],
            sec,
            other_w(d),
        )

    @pl.when(top_layer)
    def _():
        for d in range(1, ys):
            top1_in(d).wait_recv()
        for d in range(1, ws):
            top2(d).start()
        mine = pltpu.make_async_copy(
            top_rows.at[:, :, columns(w)], top_all.at[:, slab(w), :], local_s.at[1]
        )
        mine.start()
        mine.wait()

    for d in range(1, zs):
        bc2_in(d).wait_recv()
        bc3(d).start()
    own.wait()
    bc2_in(0).wait_recv()
    for d in range(1, zs):
        bc3_in(d).wait_recv()

    for g in range(ys):
        both = dot(gather, bc_all[g]).astype(BF16)
        for at in range(BLOCKS):
            start = at * block + g * run
            b_flat[start : start + run, :] = both[at * run : (at + 1) * run, 0:N]
            c_flat[start : start + run, :] = both[at * run : (at + 1) * run, N : 2 * N]

    for at in range(chunks):
        rows = slice(at * chunk, (at + 1) * chunk)
        product = lax.dot_general(
            b_flat[rows, :], c_flat[rows, :], (((1,), (1,)), ((), ())), preferred_element_type=F32
        )
        scores[rows, :] = jnp.where(col_at >= row_at, product, 0.0).astype(BF16)

    @pl.when(top_layer)
    def _():
        for d in range(1, ws):
            top2_in(d).wait_recv()
        for g in range(ys):
            ordered = dot(gather, top_all[g]).astype(BF16)
            for at in range(BLOCKS):
                start = at * block + g * run
                dy[start : start + run, :] = ordered[at * run : (at + 1) * run, :]

    def hop(at):
        rows = pl.ds(at * chunk, chunk)
        return remote(
            stream.at[rows, :],
            dy.at[rows, :],
            hop_s.at[at],
            hop_r.at[at],
            lax.rem(sec + sections - 1, sections),
            pos,
        )

    conv = [jnp.zeros((1, 2 * P_SIZE), F32) for _ in range(K)]
    for at in range(chunks - 1, -1, -1):
        rows = slice(at * chunk, (at + 1) * chunk)

        @pl.when(jnp.logical_not(top_layer))
        def _():
            hop(at).wait_recv()

        upstream = dy[rows, :].astype(F32)
        fed = (grow[rows, :] * upstream).astype(BF16)
        ended = grow[(at + 1) * chunk - 1 : (at + 1) * chunk, :] * carried[...]
        mixed = dot(scores[rows, :], fed) + dot(b_flat[rows, :], ended.astype(BF16))
        grad_pre = (shrink[rows, :] * mixed + skip * upstream) * slope[rows, :]
        extended[rows, :] = grad_pre
        grad_in = taps[0:1] * grad_pre
        for k in range(1, K):
            start = at * chunk + k
            grad_in = grad_in + taps[k : k + 1] * extended[start : start + chunk, :]
        stream[rows, :] = (upstream + grad_in.astype(BF16).astype(F32)).astype(BF16)

        @pl.when(sec > 0)
        def _():
            hop(at).start()

        carried[...] = ended + lax.dot_general(
            c_flat[rows, :], fed, (((0,), (0,)), ((), ())), preferred_element_type=F32
        )
        for k in range(K):
            start = PAD + at * chunk - k
            conv[k] = conv[k] + jnp.sum(
                grad_pre * act_pad[start : start + chunk, :], axis=0, keepdims=True
            )
    for k in range(K):
        conv_ref[k : k + 1, :] = conv[k]

    for g in range(ys):
        natural = jnp.concatenate(
            [stream[at * block + g * run : at * block + (g + 1) * run, :] for at in range(BLOCKS)],
            axis=0,
        )
        ordered = dot(scatter, natural).astype(BF16)
        for v in range(ws):
            out_send[v, g] = ordered[v * 16 : (v + 1) * 16, :]

    def out1(d):
        return remote(
            out_send.at[lax.rem(w + d, ws)],
            out_rows.at[:, :, columns(w)],
            out1_s.at[d],
            out1_r.at[d],
            sec,
            other_w(d),
        )

    def out1_in(d):
        of = lax.rem(w + ws - d, ws)
        return remote(
            out_send.at[of],
            out_rows.at[:, :, columns(of)],
            out1_s.at[d],
            out1_r.at[d],
            sec,
            other_w(d),
        )

    def wide_columns(of):
        return pl.ds(pl.multiple_of(of * wide, wide), wide)

    def out2(d):
        return remote(
            out_rows.at[lax.rem(y + d, ys)],
            out_all.at[:, wide_columns(y)],
            out2_s.at[d],
            out2_r.at[d],
            sec,
            other_y(d),
        )

    def out2_in(d):
        of = lax.rem(y + ys - d, ys)
        return remote(
            out_rows.at[of],
            out_all.at[:, wide_columns(of)],
            out2_s.at[d],
            out2_r.at[d],
            sec,
            other_y(d),
        )

    for d in range(1, ws):
        out1(d).start()
    kept = pltpu.make_async_copy(out_send.at[w], out_rows.at[:, :, columns(w)], local_s.at[2])
    kept.start()
    kept.wait()
    for d in range(1, ws):
        out1_in(d).wait_recv()
    for d in range(1, ys):
        out2(d).start()
    last = pltpu.make_async_copy(out_rows.at[y], out_all.at[:, wide_columns(y)], local_s.at[3])
    last.start()
    last.wait()

    for d in range(1, ys):
        bc1(d).wait_send()
    for d in range(zs):
        bc2(d).wait_send()
    for d in range(1, zs):
        bc3(d).wait_send()

    @pl.when(top_layer)
    def _():
        for d in range(1, ys):
            top1(d).wait_send()
        for d in range(1, ws):
            top2(d).wait_send()

    @pl.when(sec > 0)
    def _():
        for at in range(chunks):
            hop(at).wait_send()

    for d in range(1, ws):
        out1(d).wait_send()
    for d in range(1, ys):
        out2_in(d).wait_recv()
    staged[...] = out_all[...].astype(F32)
    for at in range(BLOCKS):
        out_ref[at] = staged[4 * at : 4 * at + 4, :].astype(BF16)
    for d in range(1, ys):
        out2(d).wait_send()


def on_device(
    activations, conv_weight, step_size, decay_rate, skip_gain, b_matrix, c_matrix, top_grad
):
    tensor_size = lax.axis_size("tensor")
    sections = lax.axis_size("section")
    ys = b_matrix.shape[-1] // N
    ws = tensor_size // ys
    length, width = activations.shape[1:]
    chunk = min(CHUNK, length // BLOCKS)
    chunks = length // chunk
    zs = ws // 2
    dma = pltpu.SemaphoreType.DMA
    out, conv = pl.pallas_call(
        functools.partial(kernel, (sections, ys, ws, chunk)),
        out_shape=(
            jax.ShapeDtypeStruct(top_grad.shape, BF16),
            jax.ShapeDtypeStruct((K, width), F32),
        ),
        in_specs=[pl.BlockSpec(memory_space=pltpu.VMEM)] * 8,
        out_specs=(pl.BlockSpec(memory_space=pltpu.VMEM),) * 2,
        scratch_shapes=[
            pltpu.VMEM((16, top_grad.shape[-1]), F32),
            pltpu.VMEM((ys, 16, 2 * N), BF16),
            pltpu.VMEM((ys, 16, 2 * N), BF16),
            pltpu.VMEM((ys, 16 * ws, 2 * N), BF16),
            pltpu.VMEM((ys, 16, ws * width), BF16),
            pltpu.VMEM((ys, 16, ws * width), BF16),
            pltpu.VMEM((ys, 16 * ws, width), BF16),
            pltpu.VMEM((PAD + length, width), F32),
            pltpu.VMEM((length, width), F32),
            pltpu.VMEM((length, width), F32),
            pltpu.VMEM((length, width), F32),
            pltpu.VMEM((length, N), BF16),
            pltpu.VMEM((length, N), BF16),
            pltpu.VMEM((length, chunk), BF16),
            pltpu.VMEM((N, width), F32),
            pltpu.VMEM((length, width), BF16),
            pltpu.VMEM((length, width), BF16),
            pltpu.VMEM((length + PAD, width), F32),
            pltpu.VMEM((ws, ys, 16, width), BF16),
            pltpu.VMEM((ys, 16, ws * width), BF16),
            pltpu.VMEM((16, ys * ws * width), BF16),
            dma((ys,)),
            dma((ys,)),
            dma((zs,)),
            dma((zs,)),
            dma((zs,)),
            dma((zs,)),
            dma((ys,)),
            dma((ys,)),
            dma((ws,)),
            dma((ws,)),
            dma((chunks,)),
            dma((chunks,)),
            dma((ws,)),
            dma((ws,)),
            dma((ys,)),
            dma((ys,)),
            dma((4,)),
        ],
        compiler_params=pltpu.CompilerParams(
            collective_id=0, has_side_effects=True, vmem_limit_bytes=40 * 1024 * 1024
        ),
    )(
        activations[0],
        conv_weight[0],
        step_size[0].T,
        decay_rate,
        skip_gain,
        b_matrix[0],
        c_matrix[0],
        top_grad,
    )
    return (out[None], conv[None])


def solution(mesh):
    return jax.shard_map(
        on_device,
        mesh=mesh,
        in_specs=(
            P("section", None, "tensor"),
            P("section", None, "tensor"),
            P("section", None, "tensor"),
            P("section", "tensor"),
            P("section", "tensor"),
            P("section", None, "tensor", None),
            P("section", None, "tensor", None),
            P(None, "tensor", None),
        ),
        out_specs=(P("section", None, "tensor", None), P("section", None, "tensor")),
        check_vma=False,
    )
```

```python
import functools

import jax
import jax.numpy as jnp
from jax import lax
from jax.experimental import pallas as pl
from jax.experimental.pallas import tpu as pltpu
from jax.sharding import PartitionSpec as P

P_SIZE = 64
N = 256
K = 4
BLOCKS = 4
CHUNK = 128
HALVES = 2
EARLY = 3
LAG = 3
PACED = 6
PAD = 8
F32 = jnp.float32
BF16 = jnp.bfloat16


def dot(a, b):
    return jnp.dot(a, b, preferred_element_type=F32)


def kernel(
    sizes,
    act_ref,
    taps_ref,
    step_ref,
    rate_ref,
    skip_ref,
    b_ref,
    c_ref,
    top_ref,
    out_ref,
    conv_ref,
    act_in,
    taps_in,
    step_in,
    rate_in,
    skip_in,
    bc_rows,
    bc_all,
    top_rows,
    top_all,
    top_block,
    act_pad,
    slope,
    grow,
    shrink,
    b_flat,
    c_turned,
    scores,
    carried,
    dy,
    stream,
    extended,
    out_send,
    out_rows,
    in_sem,
    bc1_s,
    bc1_r,
    bc2_s,
    bc2_r,
    bc3_r,
    top_s,
    top1_r,
    top2_r,
    hop_s,
    hop_r,
    out1_s,
    out1_r,
    out2_s,
    out2_r,
):
    sections, ys, ws, chunk, halves = sizes
    block = 4 * ys * ws
    length = BLOCKS * block
    chunks = length // chunk
    per_block = block // chunk
    per_half = per_block // halves
    ysub = ys // halves
    zs = ws // 2
    width = 2 * P_SIZE
    wide = ws * width
    sec = lax.axis_index("section")
    pos = lax.axis_index("tensor")
    y = pos // ws
    w = pos % ws
    z = w // 2
    core = w % 2
    top = sections - 1
    first_helper = sections - BLOCKS
    last_block = BLOCKS - 1
    downward = range(BLOCKS - 1, -1, -1)

    def remote(src, dst, send, recv, section, tensor):
        return pltpu.make_async_remote_copy(
            src_ref=src,
            dst_ref=dst,
            send_sem=send,
            recv_sem=recv,
            device_id=(section, tensor),
            device_id_type=pl.DeviceIdType.MESH,
        )

    def wait_bytes(like, sem):
        pltpu.make_async_copy(like, like, sem).wait()

    def columns(of, size):
        return pl.ds(pl.multiple_of(of * size, size), size)

    def to_y(d):
        return lax.rem(y + d, ys)

    def to_w(d):
        return lax.rem(w + d, ws)

    def at_y(d):
        return to_y(d) * ws + w

    def at_w(d):
        return y * ws + to_w(d)

    sibling = y * ws + z * 2 + (1 - core)
    below = lax.rem(sec + sections - 1, sections)

    fetches = [
        pltpu.make_async_copy(src, dst, in_sem.at[i])
        for i, (src, dst) in enumerate(
            (
                (act_ref, act_in),
                (taps_ref, taps_in),
                (step_ref, step_in),
                (rate_ref, rate_in),
                (skip_ref, skip_in),
            )
        )
    ]

    barrier = pltpu.get_barrier_semaphore()

    def greet(section, tensor):
        pl.semaphore_signal(
            barrier, inc=1, device_id=(section, tensor), device_id_type=pl.DeviceIdType.MESH
        )

    for d in range(1, ys):
        greet(sec, at_y(d))
    for d in range(1, ws):
        greet(sec, at_w(d))
    for d in range(1, sections):
        greet(lax.rem(sec + d, sections), pos)
    for fetch in fetches:
        fetch.start()
    pl.semaphore_wait(barrier, ys + ws + sections - 3)

    def bc1(which, d):
        return remote(
            (b_ref, c_ref)[which].at[:, :, columns(to_y(d), N)],
            bc_rows.at[y, :, which],
            bc1_s.at[0],
            bc1_r.at[0],
            sec,
            at_y(d),
        )

    for d in range(1, ys):
        for which in range(2):
            bc1(which, d).start()
    for which in range(2):
        pltpu.make_async_copy(
            (b_ref, c_ref)[which].at[:, :, columns(y, N)], bc_rows.at[y, :, which], bc1_r.at[0]
        ).start()

    helper = sec >= first_helper
    top_at = lax.max(sec - first_helper, 0)

    def top1(d):
        return remote(
            top_ref.at[top_at, :, columns(to_y(d), wide)],
            top_rows.at[y],
            top_s.at[0],
            top1_r.at[0],
            sec,
            at_y(d),
        )

    def top2(d):
        return remote(
            top_rows.at[:, :, columns(to_w(d), width)],
            top_all.at[:, w],
            top_s.at[1],
            top2_r.at[0],
            sec,
            at_w(d),
        )

    def top3(part):
        return remote(
            top_block.at[pl.ds(part * chunk, chunk), :],
            dy.at[pl.ds(pl.multiple_of(top_at * block + part * chunk, chunk), chunk), :],
            top_s.at[2],
            hop_r.at[top_at * per_block + part],
            top,
            pos,
        )

    @pl.when(helper)
    def _():
        for d in range(1, ys):
            top1(d).start()
        pltpu.make_async_copy(
            top_ref.at[top_at, :, columns(y, wide)], top_rows.at[y], top1_r.at[0]
        ).start()

    def bc2(at, d):
        to = sibling if d == 0 else y * ws + lax.rem(z + d, zs) * 2 + core
        recv = bc3_r if d == 0 else bc2_r
        return remote(bc_rows.at[:, at], bc_all.at[at, :, w], bc2_s.at[0], recv.at[at], sec, to)

    def bc3(at, d):
        piece = bc_all.at[at, :, lax.rem(z + zs - d, zs) * 2 + core]
        return remote(piece, piece, bc2_s.at[0], bc3_r.at[at], sec, sibling)

    wait_bytes(bc_rows, bc1_r.at[0])

    def spread(at):
        for d in range(zs - 1, -1, -1):
            bc2(at, d).start()
        pltpu.make_async_copy(bc_rows.at[:, at], bc_all.at[at, :, w], bc3_r.at[at]).start()

    spread(last_block)

    @pl.when(helper)
    def _():
        wait_bytes(top_rows, top1_r.at[0])
        for d in range(1, ws):
            top2(d).start()
        pltpu.make_async_copy(
            top_rows.at[:, :, columns(w, width)], top_all.at[:, w], top2_r.at[0]
        ).start()

    paced = sec >= PACED * sections // 8
    spread(last_block - 1)

    @pl.when(jnp.logical_not(paced))
    def _():
        for at in range(last_block - 2, -1, -1):
            spread(at)

    for fetch in fetches:
        fetch.wait()
    act_pad[0:PAD, :] = jnp.zeros((PAD, width), F32)
    act_pad[PAD:, :] = act_in[...].astype(F32)
    taps = taps_in[...].astype(F32)
    first = lax.broadcasted_iota(jnp.int32, (1, width), 1) < P_SIZE
    rate = jnp.where(first, rate_in[:, 0:1], rate_in[:, 1:2])
    skip = jnp.where(first, skip_in[:, 0:1], skip_in[:, 1:2])
    row_at = lax.broadcasted_iota(jnp.int32, (chunk, chunk), 0)
    col_at = lax.broadcasted_iota(jnp.int32, (chunk, chunk), 1)
    lower = (row_at >= col_at).astype(F32).astype(BF16)
    for at in range(chunks):
        rows = slice(at * chunk, (at + 1) * chunk)
        preact = jnp.zeros((chunk, width), F32)
        for k in range(K):
            start = PAD + at * chunk - k
            preact = preact + taps[k : k + 1] * act_pad[start : start + chunk, :]
        logistic = 1.0 / (1.0 + jnp.exp(-preact))
        slope_here = logistic * (1.0 + preact * (1.0 - logistic))
        step = jnp.concatenate(
            [jnp.broadcast_to(step_in[h : h + 1, rows], (P_SIZE, chunk)) for h in range(2)], axis=0
        ).T
        high = step.astype(BF16)
        rest = step - high.astype(F32)
        mid = rest.astype(BF16)
        low = (rest - mid.astype(F32)).astype(BF16)
        decay = -rate * (dot(lower, high) + dot(lower, mid) + dot(lower, low))
        grow[rows, :] = jnp.exp(decay)
        shrink[rows, :] = step * jnp.exp(-decay) * slope_here
        slope[rows, :] = skip * slope_here
    carried[...] = jnp.zeros_like(carried)
    extended[length:, :] = jnp.zeros((PAD, width), F32)

    @pl.when(helper)
    def _():
        wait_bytes(top_all, top2_r.at[0])
        gathered = top_all[...].reshape(block, width)

        @pl.when(sec == top)
        def _():
            dy[last_block * block :, :] = gathered

        @pl.when(sec != top)
        def _():
            top_block[...] = gathered
            for part in range(per_block - 1, -1, -1):
                top3(part).start()

    def hop(at):
        rows = pl.ds(at * chunk, chunk)
        return remote(
            stream.at[rows, :], dy.at[rows, :], hop_s.at[0], hop_r.at[at], below, pos
        )

    def out1(at, half, d):
        group = pl.ds(half * ysub, ysub)
        return remote(
            out_send.at[at, group, to_w(d)],
            out_rows.at[at, group, :, columns(w, width)],
            out1_s.at[0],
            out1_r.at[at * halves + half],
            sec,
            at_w(d),
        )

    def out2(at, half, d):
        to = half * ysub + lax.rem(y + d, ysub)
        return remote(
            out_rows.at[at, to],
            out_ref.at[at, :, columns(y, wide)],
            out2_s.at[0],
            out2_r.at[0],
            sec,
            to * ws + w,
        )

    def start_rows(at, half):
        group = pl.ds(half * ysub, ysub)
        begin = at * block + half * (block // halves)
        out_send[at, half * ysub : (half + 1) * ysub] = stream[
            begin : begin + block // halves, :
        ].reshape(ysub, ws, 4, width)
        for d in range(1, ws):
            out1(at, half, d).start()
        pltpu.make_async_copy(
            out_send.at[at, group, w],
            out_rows.at[at, group, :, columns(w, width)],
            out1_r.at[at * halves + half],
        ).start()

    def forward_rows(at, half):
        wait_bytes(out_rows.at[at, pl.ds(half * ysub, ysub)], out1_r.at[at * halves + half])
        for d in range(1, ysub):
            out2(at, half, d).start()
        mine = y // ysub == half

        @pl.when(mine)
        def _():
            pltpu.make_async_copy(
                out_rows.at[at, y], out_ref.at[at, :, columns(y, wide)], out2_r.at[0]
            ).start()

        @pl.when(jnp.logical_not(mine))
        def _():
            out2(at, half, 0).start()

    units = [(at, half) for at in downward for half in range(halves - 1, -1, -1)]
    done = 0
    for at in downward:
        wait_bytes(bc_all.at[at, :, 0 : zs - 1], bc2_r.at[at])
        if at >= 2:

            @pl.when(paced)
            def _():
                spread(at - 2)

        for d in range(1, zs):
            bc3(at, d).start()
        wait_bytes(bc_all.at[at, :, 0 : zs + 1], bc3_r.at[at])
        start = at * block
        b_flat[start : start + block, :] = bc_all[at, :, :, 0].reshape(block, N)
        c_here = bc_all[at, :, :, 1].reshape(block, N)
        for part in range(per_block):
            inner = slice(part * chunk, (part + 1) * chunk)
            rows = slice(start + part * chunk, start + (part + 1) * chunk)
            product = lax.dot_general(
                b_flat[rows, :], c_here[inner], (((1,), (1,)), ((), ())), preferred_element_type=F32
            )
            scores[rows, :] = jnp.where(col_at >= row_at, product, 0.0).astype(BF16)
            c_turned[at * per_block + part] = c_here[inner].T

        for part in range(per_block - 1, -1, -1):
            here = at * per_block + part
            rows = slice(here * chunk, (here + 1) * chunk)
            ended = grow[(here + 1) * chunk - 1 : (here + 1) * chunk, :] * carried[...]
            through = dot(b_flat[rows, :], ended.astype(BF16))

            if at == last_block:

                @pl.when(sec != top)
                def _():
                    hop(here).wait_recv()

            else:
                hop(here).wait_recv()

            upstream = dy[rows, :].astype(F32)
            fed = (grow[rows, :] * upstream).astype(BF16)
            mixed = dot(scores[rows, :], fed) + through
            grad_pre = shrink[rows, :] * mixed + slope[rows, :] * upstream
            extended[rows, :] = grad_pre
            grad_in = taps[0:1] * grad_pre
            for k in range(1, K):
                begin = here * chunk + k
                grad_in = grad_in + taps[k : k + 1] * extended[begin : begin + chunk, :]
            stream[rows, :] = (upstream + grad_in.astype(BF16).astype(F32)).astype(BF16)

            @pl.when(sec > 0)
            def _():
                hop(here).start()

            carried[...] = ended + dot(c_turned[here], fed)
            if part % per_half == 0:
                done += 1

                @pl.when(sec < EARLY)
                def _():
                    start_rows(*units[done - 1])
                    if done > LAG:
                        forward_rows(*units[done - 1 - LAG])

    @pl.when(sec >= EARLY)
    def _():
        for unit in units:
            start_rows(*unit)
        for unit in units[:-LAG]:
            forward_rows(*unit)

    conv = [jnp.zeros((1, width), F32) for _ in range(K)]
    for at in range(chunks):
        for k in range(K):
            start = PAD + at * chunk - k
            conv[k] = conv[k] + jnp.sum(
                extended[at * chunk : (at + 1) * chunk, :] * act_pad[start : start + chunk, :],
                axis=0,
                keepdims=True,
            )
    for k in range(K):
        conv_ref[k : k + 1, :] = conv[k]
    for unit in units[-LAG:]:
        forward_rows(*unit)

    wait_bytes(bc_rows.at[0 : ys - 1], bc1_s.at[0])
    wait_bytes(bc_all.at[:, :, 0 : 2 * zs - 1], bc2_s.at[0])

    @pl.when(helper)
    def _():
        wait_bytes(top_rows.at[0 : ys - 1], top_s.at[0])
        wait_bytes(top_all.at[:, 0 : ws - 1], top_s.at[1])

    @pl.when(helper & (sec != top))
    def _():
        wait_bytes(top_block, top_s.at[2])

    @pl.when(sec > 0)
    def _():
        wait_bytes(stream, hop_s.at[0])

    wait_bytes(out_send.at[:, :, 0 : ws - 1], out1_s.at[0])
    for at in range(BLOCKS):
        wait_bytes(out_rows.at[at, 0 : ys - 1], out2_s.at[0])
    wait_bytes(out_ref, out2_r.at[0])


def on_device(
    activations, conv_weight, step_size, decay_rate, skip_gain, b_matrix, c_matrix, top_grad
):
    tensor_size = lax.axis_size("tensor")
    sections = lax.axis_size("section")
    ys = b_matrix.shape[-1] // N
    ws = tensor_size // ys
    length, width = activations.shape[1:]
    chunk = min(CHUNK, length // BLOCKS)
    chunks = length // chunk
    halves = min(HALVES, length // BLOCKS // chunk)
    dma = pltpu.SemaphoreType.DMA
    out, conv = pl.pallas_call(
        functools.partial(kernel, (sections, ys, ws, chunk, halves)),
        out_shape=(
            jax.ShapeDtypeStruct(top_grad.shape, BF16),
            jax.ShapeDtypeStruct((K, width), F32),
        ),
        in_specs=[pl.BlockSpec(memory_space=pltpu.HBM)] * 8,
        out_specs=(pl.BlockSpec(memory_space=pltpu.VMEM),) * 2,
        scratch_shapes=[
            pltpu.VMEM((length, width), BF16),
            pltpu.VMEM((K, width), BF16),
            pltpu.VMEM((2, length), F32),
            pltpu.VMEM((1, 2), F32),
            pltpu.VMEM((1, 2), F32),
            pltpu.VMEM((ys, BLOCKS, 2, 4, N), BF16),
            pltpu.VMEM((BLOCKS, ys, ws, 2, 4, N), BF16),
            pltpu.VMEM((ys, 4, ws * width), BF16),
            pltpu.VMEM((ys, ws, 4, width), BF16),
            pltpu.VMEM((length // BLOCKS, width), BF16),
            pltpu.VMEM((PAD + length, width), F32),
            pltpu.VMEM((length, width), F32),
            pltpu.VMEM((length, width), F32),
            pltpu.VMEM((length, width), F32),
            pltpu.VMEM((length, N), BF16),
            pltpu.VMEM((chunks, N, chunk), BF16),
            pltpu.VMEM((length, chunk), BF16),
            pltpu.VMEM((N, width), F32),
            pltpu.VMEM((length, width), BF16),
            pltpu.VMEM((length, width), BF16),
            pltpu.VMEM((length + PAD, width), F32),
            pltpu.VMEM((BLOCKS, ys, ws, 4, width), BF16),
            pltpu.VMEM((BLOCKS, ys, 4, ws * width), BF16),
            dma((5,)),
            dma((1,)),
            dma((1,)),
            dma((1,)),
            dma((BLOCKS,)),
            dma((BLOCKS,)),
            dma((3,)),
            dma((1,)),
            dma((1,)),
            dma((1,)),
            dma((chunks,)),
            dma((1,)),
            dma((BLOCKS * halves,)),
            dma((1,)),
            dma((1,)),
        ],
        compiler_params=pltpu.CompilerParams(
            collective_id=0, has_side_effects=True, vmem_limit_bytes=60 * 1024 * 1024
        ),
    )(
        activations[0],
        conv_weight[0],
        step_size[0].T,
        decay_rate,
        skip_gain,
        b_matrix[0],
        c_matrix[0],
        top_grad,
    )
    return (out[None], conv[None])


def solution(mesh):
    return jax.shard_map(
        on_device,
        mesh=mesh,
        in_specs=(
            P("section", None, "tensor"),
            P("section", None, "tensor"),
            P("section", None, "tensor"),
            P("section", "tensor"),
            P("section", "tensor"),
            P("section", None, "tensor", None),
            P("section", None, "tensor", None),
            P(None, "tensor", None),
        ),
        out_specs=(P("section", None, "tensor", None), P("section", None, "tensor")),
        check_vma=False,
    )
```

```python
import functools

import jax
import jax.numpy as jnp
from jax import lax
from jax.experimental import pallas as pl
from jax.experimental.pallas import tpu as pltpu
from jax.sharding import PartitionSpec as P

P_SIZE = 64
N = 256
K = 4
BLOCKS = 4
CHUNK = 64
HALVES = 2
EARLY = 3
LAG = 3
PACED = 6
PAD = 8
F32 = jnp.float32
BF16 = jnp.bfloat16


def dot(a, b):
    return jnp.dot(a, b, preferred_element_type=F32)


def kernel(
    sizes,
    act_ref,
    taps_ref,
    step_ref,
    rate_ref,
    skip_ref,
    b_ref,
    c_ref,
    top_ref,
    out_ref,
    conv_ref,
    act_in,
    taps_in,
    step_in,
    rate_in,
    skip_in,
    bc_rows,
    bc_all,
    top_rows,
    top_all,
    top_block,
    act_pad,
    slope,
    grow,
    shrink,
    b_flat,
    c_turned,
    scores,
    carried,
    dy,
    stream,
    extended,
    out_send,
    out_rows,
    in_sem,
    bc1_s,
    bc1_r,
    bc2_s,
    bc2_r,
    bc3_r,
    top_s,
    top1_r,
    top2_r,
    hop_s,
    hop_r,
    out1_s,
    out1_r,
    out2_s,
    out2_r,
    out3_s,
    ready,
):
    sections, ys, ws, chunk, halves = sizes
    block = 4 * ys * ws
    length = BLOCKS * block
    chunks = length // chunk
    per_block = block // chunk
    per_half = per_block // halves
    ysub = ys // halves
    zs = ws // 2
    width = 2 * P_SIZE
    wide = ws * width
    sec = lax.axis_index("section")
    pos = lax.axis_index("tensor")
    y = pos // ws
    w = pos % ws
    z = w // 2
    core = w % 2
    top = sections - 1
    last_block = BLOCKS - 1
    downward = range(BLOCKS - 1, -1, -1)

    def remote(src, dst, send, recv, section, tensor):
        return pltpu.make_async_remote_copy(
            src_ref=src,
            dst_ref=dst,
            send_sem=send,
            recv_sem=recv,
            device_id=(section, tensor),
            device_id_type=pl.DeviceIdType.MESH,
        )

    def wait_bytes(like, sem):
        pltpu.make_async_copy(like, like, sem).wait()

    def columns(of, size):
        return pl.ds(pl.multiple_of(of * size, size), size)

    def to_y(d):
        return lax.rem(y + d, ys)

    def to_w(d):
        return lax.rem(w + d, ws)

    def at_y(d):
        return to_y(d) * ws + w

    def at_w(d):
        return y * ws + to_w(d)

    sibling = y * ws + z * 2 + (1 - core)
    below = lax.rem(sec + sections - 1, sections)

    fetches = [
        pltpu.make_async_copy(src, dst, in_sem.at[i])
        for i, (src, dst) in enumerate(
            (
                (act_ref, act_in),
                (taps_ref, taps_in),
                (step_ref, step_in),
                (rate_ref, rate_in),
                (skip_ref, skip_in),
            )
        )
    ]

    barrier = pltpu.get_barrier_semaphore()

    def greet(section, tensor):
        pl.semaphore_signal(
            barrier, inc=1, device_id=(section, tensor), device_id_type=pl.DeviceIdType.MESH
        )

    for d in range(1, ys):
        greet(sec, at_y(d))
    for d in range(1, ws):
        greet(sec, at_w(d))

    @pl.when(sec < top)
    def _():
        greet(sec + 1, pos)

    @pl.when(sec < BLOCKS)
    def _():
        greet(top, pos)

    for fetch in fetches:
        fetch.start()
    below_greets = jnp.where(sec > 0, 1, 0)
    helpers_greet = jnp.where(sec == top, BLOCKS, 0)
    pl.semaphore_wait(barrier, ys + ws - 2 + below_greets + helpers_greet)

    @pl.when(sec == top)
    def _():
        for to in range(BLOCKS):
            pl.semaphore_signal(
                ready.at[0], inc=1, device_id=(to, pos), device_id_type=pl.DeviceIdType.MESH
            )


    helper = sec < BLOCKS
    top_at = jnp.where(sec == 3, 0, jnp.where(sec == 2, 3, jnp.where(sec == 1, 1, 2)))

    def top1(d):
        return remote(
            top_ref.at[top_at, :, columns(to_y(d), wide)],
            top_rows.at[y],
            top_s.at[0],
            top1_r.at[0],
            sec,
            at_y(d),
        )

    def top2(d):
        return remote(
            top_rows.at[:, :, columns(to_w(d), width)],
            top_all.at[:, w],
            top_s.at[1],
            top2_r.at[0],
            sec,
            at_w(d),
        )

    def top3(part):
        return remote(
            top_block.at[pl.ds(part * chunk, chunk), :],
            dy.at[pl.ds(pl.multiple_of(top_at * block + part * chunk, chunk), chunk), :],
            top_s.at[2],
            hop_r.at[top_at * per_block + part],
            top,
            pos,
        )

    @pl.when(helper)
    def _():
        for d in range(1, ys):
            top1(d).start()
        pltpu.make_async_copy(
            top_ref.at[top_at, :, columns(y, wide)], top_rows.at[y], top1_r.at[0]
        ).start()

    def bc1(at, which, d):
        return remote(
            (b_ref, c_ref)[which].at[at, :, columns(to_y(d), N)],
            bc_rows.at[y, at, which],
            bc1_s.at[0],
            bc1_r.at[at],
            sec,
            at_y(d),
        )

    for at in downward:
        for d in range(1, ys):
            for which in range(2):
                bc1(at, which, d).start()
        for which in range(2):
            pltpu.make_async_copy(
                (b_ref, c_ref)[which].at[at, :, columns(y, N)],
                bc_rows.at[y, at, which],
                bc1_r.at[at],
            ).start()

    @pl.when(helper)
    def _():
        wait_bytes(top_rows, top1_r.at[0])
        for d in range(1, ws):
            top2(d).start()
        pltpu.make_async_copy(
            top_rows.at[:, :, columns(w, width)], top_all.at[:, w], top2_r.at[0]
        ).start()

    def bc2(at, d):
        to = sibling if d == 0 else y * ws + lax.rem(z + d, zs) * 2 + core
        recv = bc3_r if d == 0 else bc2_r
        return remote(bc_rows.at[:, at], bc_all.at[at, :, w], bc2_s.at[0], recv.at[at], sec, to)

    def bc3(at, d):
        piece = bc_all.at[at, :, lax.rem(z + zs - d, zs) * 2 + core]
        return remote(piece, piece, bc2_s.at[0], bc3_r.at[at], sec, sibling)

    def spread(at):
        for d in range(zs - 1, -1, -1):
            bc2(at, d).start()
        pltpu.make_async_copy(bc_rows.at[:, at], bc_all.at[at, :, w], bc3_r.at[at]).start()

    paced = sec >= PACED * sections // 8

    def collect(at):
        wait_bytes(bc_all.at[at, :, 0 : zs - 1], bc2_r.at[at])

        if at >= 2:

            @pl.when(paced)
            def _():
                spread(at - 2)

        for d in range(1, zs):
            bc3(at, d).start()

    wait_bytes(bc_rows.at[:, last_block], bc1_r.at[last_block])
    spread(last_block)

    for fetch in fetches:
        fetch.wait()
    act_pad[0:PAD, :] = jnp.zeros((PAD, width), F32)
    act_pad[PAD:, :] = act_in[...].astype(F32)
    taps = taps_in[...].astype(F32)
    first = lax.broadcasted_iota(jnp.int32, (1, width), 1) < P_SIZE
    rate = jnp.where(first, rate_in[:, 0:1], rate_in[:, 1:2])
    skip = jnp.where(first, skip_in[:, 0:1], skip_in[:, 1:2])
    row_at = lax.broadcasted_iota(jnp.int32, (chunk, chunk), 0)
    col_at = lax.broadcasted_iota(jnp.int32, (chunk, chunk), 1)
    lower = (row_at >= col_at).astype(F32).astype(BF16)
    for at in range(chunks):
        rows = slice(at * chunk, (at + 1) * chunk)
        preact = jnp.zeros((chunk, width), F32)
        for k in range(K):
            start = PAD + at * chunk - k
            preact = preact + taps[k : k + 1] * act_pad[start : start + chunk, :]
        logistic = 1.0 / (1.0 + jnp.exp(-preact))
        slope_here = logistic * (1.0 + preact * (1.0 - logistic))
        step = jnp.concatenate(
            [jnp.broadcast_to(step_in[h : h + 1, rows], (P_SIZE, chunk)) for h in range(2)], axis=0
        ).T
        high = step.astype(BF16)
        rest = step - high.astype(F32)
        mid = rest.astype(BF16)
        low = (rest - mid.astype(F32)).astype(BF16)
        decay = -rate * (dot(lower, high) + dot(lower, mid) + dot(lower, low))
        grow[rows, :] = jnp.exp(decay)
        shrink[rows, :] = step * jnp.exp(-decay) * slope_here
        slope[rows, :] = skip * slope_here
    carried[...] = jnp.zeros_like(carried)
    extended[length:, :] = jnp.zeros((PAD, width), F32)

    wait_bytes(bc_rows.at[:, last_block - 1], bc1_r.at[last_block - 1])
    spread(last_block - 1)
    for at in range(last_block - 2, -1, -1):
        wait_bytes(bc_rows.at[:, at], bc1_r.at[at])

    @pl.when(jnp.logical_not(paced))
    def _():
        for at in range(last_block - 2, -1, -1):
            spread(at)

    @pl.when(helper)
    def _():
        wait_bytes(top_all, top2_r.at[0])
        gathered = top_all[...].reshape(block, width)

        top_block[...] = gathered
        pl.semaphore_wait(ready.at[0], 1)
        for part in range(per_block - 1, -1, -1):
            top3(part).start()

    @pl.when(jnp.logical_not(paced))
    def _():
        for at in downward:
            collect(at)

    def hop(at):
        rows = pl.ds(at * chunk, chunk)
        return remote(
            stream.at[rows, :], dy.at[rows, :], hop_s.at[0], hop_r.at[at], below, pos
        )

    def out1(at, half, d):
        group = pl.ds(half * ysub, ysub)
        return remote(
            out_send.at[at, group, to_w(d)],
            out_rows.at[at, group, :, columns(w, width)],
            out1_s.at[0],
            out1_r.at[at * halves + half],
            sec,
            at_w(d),
        )

    def out2(at, half, d):
        to = half * ysub + lax.rem(y + d, ysub)
        return remote(
            out_rows.at[at, to],
            out_ref.at[at, :, columns(y, wide)],
            out2_s.at[0],
            out2_r.at[0],
            sec,
            to * ws + w,
        )

    def out3(to, d):
        return remote(
            out_send.at[0, to, to_w(d)],
            out_ref.at[0, :, columns(pos, width)],
            out3_s.at[0 if d else 1],
            out2_r.at[0],
            sec,
            to * ws + to_w(d),
        )

    def send_last():
        out_send[0, 0:ysub] = stream[0 : block // halves, :].reshape(ysub, ws, 4, width)
        for to in range(ysub):
            for d in range(1, ws):
                out3(to, d).start()

            @pl.when(y == to)
            def _():
                pltpu.make_async_copy(
                    out_send.at[0, to, w], out_ref.at[0, :, columns(pos, width)], out2_r.at[0]
                ).start()

            @pl.when(y != to)
            def _():
                out3(to, 0).start()

    def start_rows(at, half):
        group = pl.ds(half * ysub, ysub)
        begin = at * block + half * (block // halves)
        out_send[at, half * ysub : (half + 1) * ysub] = stream[
            begin : begin + block // halves, :
        ].reshape(ysub, ws, 4, width)
        for d in range(1, ws):
            out1(at, half, d).start()
        pltpu.make_async_copy(
            out_send.at[at, group, w],
            out_rows.at[at, group, :, columns(w, width)],
            out1_r.at[at * halves + half],
        ).start()

    def forward_rows(at, half):
        wait_bytes(out_rows.at[at, pl.ds(half * ysub, ysub)], out1_r.at[at * halves + half])
        for d in range(1, ysub):
            out2(at, half, d).start()
        mine = y // ysub == half

        @pl.when(mine)
        def _():
            pltpu.make_async_copy(
                out_rows.at[at, y], out_ref.at[at, :, columns(y, wide)], out2_r.at[0]
            ).start()

        @pl.when(jnp.logical_not(mine))
        def _():
            out2(at, half, 0).start()

    units = [(at, half) for at in downward for half in range(halves - 1, -1, -1)]
    done = 0
    for at in downward:
        @pl.when(paced)
        def _():
            collect(at)

        wait_bytes(bc_all.at[at, :, 0 : zs + 1], bc3_r.at[at])
        start = at * block
        b_flat[start : start + block, :] = bc_all[at, :, :, 0].reshape(block, N)
        c_here = bc_all[at, :, :, 1].reshape(block, N)
        for part in range(per_block):
            inner = slice(part * chunk, (part + 1) * chunk)
            rows = slice(start + part * chunk, start + (part + 1) * chunk)
            product = lax.dot_general(
                b_flat[rows, :], c_here[inner], (((1,), (1,)), ((), ())), preferred_element_type=F32
            )
            scores[rows, :] = jnp.where(col_at >= row_at, product, 0.0).astype(BF16)
            c_turned[at * per_block + part] = c_here[inner].T

        for part in range(per_block - 1, -1, -1):
            here = at * per_block + part
            rows = slice(here * chunk, (here + 1) * chunk)
            ended = grow[(here + 1) * chunk - 1 : (here + 1) * chunk, :] * carried[...]
            through = dot(b_flat[rows, :], ended.astype(BF16))

            hop(here).wait_recv()
            upstream = dy[rows, :].astype(F32)
            fed = (grow[rows, :] * upstream).astype(BF16)
            mixed = dot(scores[rows, :], fed) + through
            grad_pre = shrink[rows, :] * mixed + slope[rows, :] * upstream
            extended[rows, :] = grad_pre
            grad_in = taps[0:1] * grad_pre
            for k in range(1, K):
                begin = here * chunk + k
                grad_in = grad_in + taps[k : k + 1] * extended[begin : begin + chunk, :]
            stream[rows, :] = (upstream + grad_in.astype(BF16).astype(F32)).astype(BF16)

            @pl.when(sec > 0)
            def _():
                hop(here).start()

            carried[...] = ended + dot(c_turned[here], fed)
            if part % per_half == 0:
                done += 1

                @pl.when(sec < EARLY)
                def _():
                    if done < len(units):
                        start_rows(*units[done - 1])
                    else:
                        send_last()
                    if done > LAG:
                        forward_rows(*units[done - 1 - LAG])

    @pl.when(sec >= EARLY)
    def _():
        for unit in units[:-1]:
            start_rows(*unit)
        send_last()
        for unit in units[:-LAG]:
            forward_rows(*unit)

    for unit in units[-LAG:-1]:
        forward_rows(*unit)

    conv = [jnp.zeros((1, width), F32) for _ in range(K)]
    for at in range(chunks):
        for k in range(K):
            start = PAD + at * chunk - k
            conv[k] = conv[k] + jnp.sum(
                extended[at * chunk : (at + 1) * chunk, :] * act_pad[start : start + chunk, :],
                axis=0,
                keepdims=True,
            )
    for k in range(K):
        conv_ref[k : k + 1, :] = conv[k]

    wait_bytes(bc_rows.at[0 : ys - 1], bc1_s.at[0])
    wait_bytes(bc_all.at[:, :, 0 : 2 * zs - 1], bc2_s.at[0])

    @pl.when(helper)
    def _():
        wait_bytes(top_rows.at[0 : ys - 1], top_s.at[0])
        wait_bytes(top_all.at[:, 0 : ws - 1], top_s.at[1])
        wait_bytes(top_block, top_s.at[2])

    @pl.when(sec > 0)
    def _():
        wait_bytes(stream, hop_s.at[0])

    wait_bytes(out_send.at[1:BLOCKS, :, 0 : ws - 1], out1_s.at[0])
    wait_bytes(out_send.at[0, ysub:ys, 0 : ws - 1], out1_s.at[0])
    for at in range(1, BLOCKS):
        wait_bytes(out_rows.at[at, 0 : ys - 1], out2_s.at[0])
    wait_bytes(out_send.at[0, 0:ysub, 0 : ws - 1], out3_s.at[0])
    in_last = y // ysub == 0

    @pl.when(in_last)
    def _():
        wait_bytes(out_rows.at[0, 0 : ys - ysub], out2_s.at[0])
        wait_bytes(out_send.at[0, 0 : ysub - 1, 0], out3_s.at[1])

    @pl.when(jnp.logical_not(in_last))
    def _():
        wait_bytes(out_rows.at[0, 0 : ysub - 1], out2_s.at[0])
        wait_bytes(out_send.at[0, 0:ysub, 0], out3_s.at[1])

    wait_bytes(out_ref, out2_r.at[0])


def on_device(
    activations, conv_weight, step_size, decay_rate, skip_gain, b_matrix, c_matrix, top_grad
):
    tensor_size = lax.axis_size("tensor")
    sections = lax.axis_size("section")
    ys = b_matrix.shape[-1] // N
    ws = tensor_size // ys
    length, width = activations.shape[1:]
    chunk = min(CHUNK, length // BLOCKS)
    chunks = length // chunk
    halves = min(HALVES, length // BLOCKS // chunk)
    dma = pltpu.SemaphoreType.DMA
    out, conv = pl.pallas_call(
        functools.partial(kernel, (sections, ys, ws, chunk, halves)),
        out_shape=(
            jax.ShapeDtypeStruct(top_grad.shape, BF16),
            jax.ShapeDtypeStruct((K, width), F32),
        ),
        in_specs=[pl.BlockSpec(memory_space=pltpu.HBM)] * 8,
        out_specs=(pl.BlockSpec(memory_space=pltpu.VMEM),) * 2,
        scratch_shapes=[
            pltpu.VMEM((length, width), BF16),
            pltpu.VMEM((K, width), BF16),
            pltpu.VMEM((2, length), F32),
            pltpu.VMEM((1, 2), F32),
            pltpu.VMEM((1, 2), F32),
            pltpu.VMEM((ys, BLOCKS, 2, 4, N), BF16),
            pltpu.VMEM((BLOCKS, ys, ws, 2, 4, N), BF16),
            pltpu.VMEM((ys, 4, ws * width), BF16),
            pltpu.VMEM((ys, ws, 4, width), BF16),
            pltpu.VMEM((length // BLOCKS, width), BF16),
            pltpu.VMEM((PAD + length, width), F32),
            pltpu.VMEM((length, width), F32),
            pltpu.VMEM((length, width), F32),
            pltpu.VMEM((length, width), F32),
            pltpu.VMEM((length, N), BF16),
            pltpu.VMEM((chunks, N, chunk), BF16),
            pltpu.VMEM((length, chunk), BF16),
            pltpu.VMEM((N, width), F32),
            pltpu.VMEM((length, width), BF16),
            pltpu.VMEM((length, width), BF16),
            pltpu.VMEM((length + PAD, width), F32),
            pltpu.VMEM((BLOCKS, ys, ws, 4, width), BF16),
            pltpu.VMEM((BLOCKS, ys, 4, ws * width), BF16),
            dma((5,)),
            dma((1,)),
            dma((BLOCKS,)),
            dma((1,)),
            dma((BLOCKS,)),
            dma((BLOCKS,)),
            dma((3,)),
            dma((1,)),
            dma((1,)),
            dma((1,)),
            dma((chunks,)),
            dma((1,)),
            dma((BLOCKS * halves,)),
            dma((1,)),
            dma((1,)),
            dma((2,)),
            pltpu.SemaphoreType.REGULAR((1,)),
        ],
        compiler_params=pltpu.CompilerParams(
            collective_id=0, has_side_effects=True, vmem_limit_bytes=60 * 1024 * 1024
        ),
    )(
        activations[0],
        conv_weight[0],
        step_size[0].T,
        decay_rate,
        skip_gain,
        b_matrix[0],
        c_matrix[0],
        top_grad,
    )
    return (out[None], conv[None])


def solution(mesh):
    return jax.shard_map(
        on_device,
        mesh=mesh,
        in_specs=(
            P("section", None, "tensor"),
            P("section", None, "tensor"),
            P("section", None, "tensor"),
            P("section", "tensor"),
            P("section", "tensor"),
            P("section", None, "tensor", None),
            P("section", None, "tensor", None),
            P(None, "tensor", None),
        ),
        out_specs=(P("section", None, "tensor", None), P("section", None, "tensor")),
        check_vma=False,
    )
```

```python
import functools

import jax
import jax.numpy as jnp
from jax import lax
from jax.experimental import pallas as pl
from jax.experimental.pallas import tpu as pltpu
from jax.sharding import PartitionSpec as P

P_SIZE = 64
N = 256
K = 4
BLOCKS = 4
CHUNK = 64
HALVES = 2
EARLY = 3
LAG = 3
PACED = 6
PAD = 8
F32 = jnp.float32
BF16 = jnp.bfloat16


def dot(a, b):
    return jnp.dot(a, b, preferred_element_type=F32)


def kernel(
    sizes,
    act_ref,
    taps_ref,
    step_ref,
    rate_ref,
    skip_ref,
    b_ref,
    c_ref,
    top_ref,
    out_ref,
    conv_ref,
    act_in,
    taps_in,
    step_in,
    rate_in,
    skip_in,
    bc_rows,
    bc_all,
    top_rows,
    top_all,
    top_block,
    act_pad,
    slope,
    grow,
    shrink,
    b_flat,
    c_turned,
    scores,
    carried,
    dy,
    stream,
    extended,
    out_send,
    out_rows,
    in_sem,
    bc1_s,
    bc1_r,
    bc2_s,
    bc2_r,
    bc3_r,
    top_s,
    top1_r,
    top2_r,
    hop_s,
    hop_r,
    out1_s,
    out1_r,
    out2_s,
    out2_r,
    out3_s,
    ready,
):
    sections, ys, ws, chunk, halves = sizes
    block = 4 * ys * ws
    length = BLOCKS * block
    chunks = length // chunk
    per_block = block // chunk
    per_half = per_block // halves
    ysub = ys // halves
    zs = ws // 2
    width = 2 * P_SIZE
    wide = ws * width
    sec = lax.axis_index("section")
    pos = lax.axis_index("tensor")
    y = pos // ws
    w = pos % ws
    z = w // 2
    core = w % 2
    top = sections - 1
    last_block = BLOCKS - 1
    downward = range(BLOCKS - 1, -1, -1)

    def remote(src, dst, send, recv, section, tensor):
        return pltpu.make_async_remote_copy(
            src_ref=src,
            dst_ref=dst,
            send_sem=send,
            recv_sem=recv,
            device_id=(section, tensor),
            device_id_type=pl.DeviceIdType.MESH,
        )

    def wait_bytes(like, sem):
        pltpu.make_async_copy(like, like, sem).wait()

    def columns(of, size):
        return pl.ds(pl.multiple_of(of * size, size), size)

    def to_y(d):
        return lax.rem(y + d, ys)

    def to_w(d):
        return lax.rem(w + d, ws)

    def at_y(d):
        return to_y(d) * ws + w

    def at_w(d):
        return y * ws + to_w(d)

    sibling = y * ws + z * 2 + (1 - core)
    below = lax.rem(sec + sections - 1, sections)

    fetches = [
        pltpu.make_async_copy(src, dst, in_sem.at[i])
        for i, (src, dst) in enumerate(
            (
                (act_ref, act_in),
                (taps_ref, taps_in),
                (step_ref, step_in),
                (rate_ref, rate_in),
                (skip_ref, skip_in),
            )
        )
    ]

    barrier = pltpu.get_barrier_semaphore()

    def greet(section, tensor):
        pl.semaphore_signal(
            barrier, inc=1, device_id=(section, tensor), device_id_type=pl.DeviceIdType.MESH
        )

    for d in range(1, ys):
        greet(sec, at_y(d))
    for d in range(1, ws):
        greet(sec, at_w(d))

    @pl.when(sec < top)
    def _():
        greet(sec + 1, pos)

    @pl.when(sec < BLOCKS)
    def _():
        greet(top, pos)

    for fetch in fetches:
        fetch.start()
    below_greets = jnp.where(sec > 0, 1, 0)
    helpers_greet = jnp.where(sec == top, BLOCKS, 0)
    pl.semaphore_wait(barrier, ys + ws - 2 + below_greets + helpers_greet)

    @pl.when(sec == top)
    def _():
        for to in range(BLOCKS):
            pl.semaphore_signal(
                ready.at[0], inc=1, device_id=(to, pos), device_id_type=pl.DeviceIdType.MESH
            )


    helper = sec < BLOCKS
    top_at = jnp.where(sec == 3, 0, jnp.where(sec == 2, 3, jnp.where(sec == 1, 1, 2)))

    def top1(d):
        return remote(
            top_ref.at[top_at, :, columns(to_y(d), wide)],
            top_rows.at[y],
            top_s.at[0],
            top1_r.at[0],
            sec,
            at_y(d),
        )

    def top2(d):
        return remote(
            top_rows.at[:, :, columns(to_w(d), width)],
            top_all.at[:, w],
            top_s.at[1],
            top2_r.at[0],
            sec,
            at_w(d),
        )

    def top3(part):
        return remote(
            top_block.at[pl.ds(part * chunk, chunk), :],
            dy.at[pl.ds(pl.multiple_of(top_at * block + part * chunk, chunk), chunk), :],
            top_s.at[2],
            hop_r.at[top_at * per_block + part],
            top,
            pos,
        )

    @pl.when(helper)
    def _():
        for d in range(1, ys):
            top1(d).start()
        pltpu.make_async_copy(
            top_ref.at[top_at, :, columns(y, wide)], top_rows.at[y], top1_r.at[0]
        ).start()

    def bc1(at, which, d):
        return remote(
            (b_ref, c_ref)[which].at[at, :, columns(to_y(d), N)],
            bc_rows.at[y, at, which],
            bc1_s.at[0],
            bc1_r.at[at],
            sec,
            at_y(d),
        )

    for at in downward:
        for d in range(1, ys):
            for which in range(2):
                bc1(at, which, d).start()
        for which in range(2):
            pltpu.make_async_copy(
                (b_ref, c_ref)[which].at[at, :, columns(y, N)],
                bc_rows.at[y, at, which],
                bc1_r.at[at],
            ).start()

    @pl.when(helper)
    def _():
        wait_bytes(top_rows, top1_r.at[0])
        for d in range(1, ws):
            top2(d).start()
        pltpu.make_async_copy(
            top_rows.at[:, :, columns(w, width)], top_all.at[:, w], top2_r.at[0]
        ).start()

    def bc2(at, d):
        to = sibling if d == 0 else y * ws + lax.rem(z + d, zs) * 2 + core
        recv = bc3_r if d == 0 else bc2_r
        return remote(bc_rows.at[:, at], bc_all.at[at, :, w], bc2_s.at[0], recv.at[at], sec, to)

    def bc3(at, d):
        piece = bc_all.at[at, :, lax.rem(z + zs - d, zs) * 2 + core]
        return remote(piece, piece, bc2_s.at[0], bc3_r.at[at], sec, sibling)

    def spread(at):
        for d in range(zs - 1, -1, -1):
            bc2(at, d).start()
        pltpu.make_async_copy(bc_rows.at[:, at], bc_all.at[at, :, w], bc3_r.at[at]).start()

    paced = sec >= PACED * sections // 8

    def collect(at):
        wait_bytes(bc_all.at[at, :, 0 : zs - 1], bc2_r.at[at])

        if at >= 2:

            @pl.when(paced)
            def _():
                spread(at - 2)

        for d in range(1, zs):
            bc3(at, d).start()

    wait_bytes(bc_rows.at[:, last_block], bc1_r.at[last_block])
    spread(last_block)

    for fetch in fetches:
        fetch.wait()
    act_pad[0:PAD, :] = jnp.zeros((PAD, width), F32)
    act_pad[PAD:, :] = act_in[...].astype(F32)
    taps = taps_in[...].astype(F32)
    first = lax.broadcasted_iota(jnp.int32, (1, width), 1) < P_SIZE
    rate = jnp.where(first, rate_in[:, 0:1], rate_in[:, 1:2])
    skip = jnp.where(first, skip_in[:, 0:1], skip_in[:, 1:2])
    row_at = lax.broadcasted_iota(jnp.int32, (chunk, chunk), 0)
    col_at = lax.broadcasted_iota(jnp.int32, (chunk, chunk), 1)
    lower = (row_at >= col_at).astype(F32).astype(BF16)
    for at in range(chunks):
        rows = slice(at * chunk, (at + 1) * chunk)
        preact = jnp.zeros((chunk, width), F32)
        for k in range(K):
            start = PAD + at * chunk - k
            preact = preact + taps[k : k + 1] * act_pad[start : start + chunk, :]
        logistic = 1.0 / (1.0 + jnp.exp(-preact))
        slope_here = logistic * (1.0 + preact * (1.0 - logistic))
        step = jnp.concatenate(
            [jnp.broadcast_to(step_in[h : h + 1, rows], (P_SIZE, chunk)) for h in range(2)], axis=0
        ).T
        high = step.astype(BF16)
        rest = step - high.astype(F32)
        mid = rest.astype(BF16)
        low = (rest - mid.astype(F32)).astype(BF16)
        decay = -rate * (dot(lower, high) + dot(lower, mid) + dot(lower, low))
        grow[rows, :] = jnp.exp(decay)
        shrink[rows, :] = step * jnp.exp(-decay) * slope_here
        slope[rows, :] = skip * slope_here
    carried[...] = jnp.zeros_like(carried)
    extended[length:, :] = jnp.zeros((PAD, width), F32)

    wait_bytes(bc_rows.at[:, last_block - 1], bc1_r.at[last_block - 1])
    spread(last_block - 1)
    for at in range(last_block - 2, -1, -1):
        wait_bytes(bc_rows.at[:, at], bc1_r.at[at])

    @pl.when(jnp.logical_not(paced))
    def _():
        for at in range(last_block - 2, -1, -1):
            spread(at)

    @pl.when(helper)
    def _():
        wait_bytes(top_all, top2_r.at[0])
        gathered = top_all[...].reshape(block, width)

        top_block[...] = gathered
        pl.semaphore_wait(ready.at[0], 1)
        for part in range(per_block - 1, -1, -1):
            top3(part).start()

    @pl.when(jnp.logical_not(paced))
    def _():
        for at in downward:
            collect(at)

    def hop(at):
        rows = pl.ds(at * chunk, chunk)
        return remote(
            stream.at[rows, :], dy.at[rows, :], hop_s.at[0], hop_r.at[at], below, pos
        )

    def out1(at, half, d):
        group = pl.ds(half * ysub, ysub)
        return remote(
            out_send.at[at, group, to_w(d)],
            out_rows.at[at, group, :, columns(w, width)],
            out1_s.at[0],
            out1_r.at[at * halves + half],
            sec,
            at_w(d),
        )

    def out2(at, half, d):
        to = half * ysub + lax.rem(y + d, ysub)
        return remote(
            out_rows.at[at, to],
            out_ref.at[at, :, columns(y, wide)],
            out2_s.at[0],
            out2_r.at[0],
            sec,
            to * ws + w,
        )

    def out3(to, d):
        return remote(
            out_send.at[0, to, to_w(d)],
            out_ref.at[0, :, columns(pos, width)],
            out3_s.at[0 if d else 1],
            out2_r.at[0],
            sec,
            to * ws + to_w(d),
        )

    def send_last():
        out_send[0, 0:ysub] = stream[0 : block // halves, :].reshape(ysub, ws, 4, width)
        for to in range(ysub):
            for d in range(1, ws):
                out3(to, d).start()

            @pl.when(y == to)
            def _():
                pltpu.make_async_copy(
                    out_send.at[0, to, w], out_ref.at[0, :, columns(pos, width)], out2_r.at[0]
                ).start()

            @pl.when(y != to)
            def _():
                out3(to, 0).start()

    def start_rows(at, half):
        group = pl.ds(half * ysub, ysub)
        begin = at * block + half * (block // halves)
        out_send[at, half * ysub : (half + 1) * ysub] = stream[
            begin : begin + block // halves, :
        ].reshape(ysub, ws, 4, width)
        for d in range(1, ws):
            out1(at, half, d).start()
        pltpu.make_async_copy(
            out_send.at[at, group, w],
            out_rows.at[at, group, :, columns(w, width)],
            out1_r.at[at * halves + half],
        ).start()

    def forward_rows(at, half):
        wait_bytes(out_rows.at[at, pl.ds(half * ysub, ysub)], out1_r.at[at * halves + half])
        for d in range(1, ysub):
            out2(at, half, d).start()
        mine = y // ysub == half

        @pl.when(mine)
        def _():
            pltpu.make_async_copy(
                out_rows.at[at, y], out_ref.at[at, :, columns(y, wide)], out2_r.at[0]
            ).start()

        @pl.when(jnp.logical_not(mine))
        def _():
            out2(at, half, 0).start()

    units = [(at, half) for at in downward for half in range(halves - 1, -1, -1)]
    done = 0
    for at in downward:
        @pl.when(paced)
        def _():
            collect(at)

        wait_bytes(bc_all.at[at, :, 0 : zs + 1], bc3_r.at[at])
        start = at * block
        b_flat[start : start + block, :] = bc_all[at, :, :, 0].reshape(block, N)
        c_here = bc_all[at, :, :, 1].reshape(block, N)
        for part in range(per_block):
            inner = slice(part * chunk, (part + 1) * chunk)
            rows = slice(start + part * chunk, start + (part + 1) * chunk)
            product = lax.dot_general(
                b_flat[rows, :], c_here[inner], (((1,), (1,)), ((), ())), preferred_element_type=F32
            )
            scores[rows, :] = jnp.where(col_at >= row_at, product, 0.0).astype(BF16)
            c_turned[at * per_block + part] = c_here[inner].T

        for part in range(per_block - 1, -1, -1):
            here = at * per_block + part
            rows = slice(here * chunk, (here + 1) * chunk)
            ended = grow[(here + 1) * chunk - 1 : (here + 1) * chunk, :] * carried[...]
            through = dot(b_flat[rows, :], ended.astype(BF16))

            hop(here).wait_recv()
            upstream = dy[rows, :].astype(F32)
            fed = (grow[rows, :] * upstream).astype(BF16)
            mixed = dot(scores[rows, :], fed) + through
            grad_pre = shrink[rows, :] * mixed + slope[rows, :] * upstream
            extended[rows, :] = grad_pre
            grad_in = taps[0:1] * grad_pre
            for k in range(1, K):
                begin = here * chunk + k
                grad_in = grad_in + taps[k : k + 1] * extended[begin : begin + chunk, :]
            stream[rows, :] = (upstream + grad_in.astype(BF16).astype(F32)).astype(BF16)

            @pl.when(sec > 0)
            def _():
                hop(here).start()

            carried[...] = ended + dot(c_turned[here], fed)
            if part % per_half == 0:
                done += 1

                @pl.when(sec < EARLY)
                def _():
                    if done < len(units):
                        start_rows(*units[done - 1])
                    else:
                        send_last()
                    if done > LAG:
                        forward_rows(*units[done - 1 - LAG])

    @pl.when(sec >= EARLY)
    def _():
        for unit in units[:-1]:
            start_rows(*unit)
        send_last()
        for unit in units[:-LAG]:
            forward_rows(*unit)

    for unit in units[-LAG:-1]:
        forward_rows(*unit)

    conv = [jnp.zeros((1, width), F32) for _ in range(K)]
    for at in range(chunks):
        for k in range(K):
            start = PAD + at * chunk - k
            conv[k] = conv[k] + jnp.sum(
                extended[at * chunk : (at + 1) * chunk, :] * act_pad[start : start + chunk, :],
                axis=0,
                keepdims=True,
            )
    for k in range(K):
        conv_ref[k : k + 1, :] = conv[k]

    wait_bytes(bc_rows.at[0 : ys - 1], bc1_s.at[0])
    wait_bytes(bc_all.at[:, :, 0 : 2 * zs - 1], bc2_s.at[0])

    @pl.when(helper)
    def _():
        wait_bytes(top_rows.at[0 : ys - 1], top_s.at[0])
        wait_bytes(top_all.at[:, 0 : ws - 1], top_s.at[1])
        wait_bytes(top_block, top_s.at[2])

    @pl.when(sec > 0)
    def _():
        wait_bytes(stream, hop_s.at[0])

    wait_bytes(out_send.at[1:BLOCKS, :, 0 : ws - 1], out1_s.at[0])
    wait_bytes(out_send.at[0, ysub:ys, 0 : ws - 1], out1_s.at[0])
    for at in range(1, BLOCKS):
        wait_bytes(out_rows.at[at, 0 : ys - 1], out2_s.at[0])
    wait_bytes(out_send.at[0, 0:ysub, 0 : ws - 1], out3_s.at[0])
    in_last = y // ysub == 0

    @pl.when(in_last)
    def _():
        wait_bytes(out_rows.at[0, 0 : ys - ysub], out2_s.at[0])
        wait_bytes(out_send.at[0, 0 : ysub - 1, 0], out3_s.at[1])

    @pl.when(jnp.logical_not(in_last))
    def _():
        wait_bytes(out_rows.at[0, 0 : ys - ysub - 1], out2_s.at[0])
        wait_bytes(out_send.at[0, 0:ysub, 0], out3_s.at[1])

    wait_bytes(out_ref, out2_r.at[0])


def on_device(
    activations, conv_weight, step_size, decay_rate, skip_gain, b_matrix, c_matrix, top_grad
):
    tensor_size = lax.axis_size("tensor")
    sections = lax.axis_size("section")
    ys = b_matrix.shape[-1] // N
    ws = tensor_size // ys
    length, width = activations.shape[1:]
    chunk = min(CHUNK, length // BLOCKS)
    chunks = length // chunk
    halves = min(HALVES, length // BLOCKS // chunk)
    dma = pltpu.SemaphoreType.DMA
    out, conv = pl.pallas_call(
        functools.partial(kernel, (sections, ys, ws, chunk, halves)),
        out_shape=(
            jax.ShapeDtypeStruct(top_grad.shape, BF16),
            jax.ShapeDtypeStruct((K, width), F32),
        ),
        in_specs=[pl.BlockSpec(memory_space=pltpu.HBM)] * 8,
        out_specs=(pl.BlockSpec(memory_space=pltpu.VMEM),) * 2,
        scratch_shapes=[
            pltpu.VMEM((length, width), BF16),
            pltpu.VMEM((K, width), BF16),
            pltpu.VMEM((2, length), F32),
            pltpu.VMEM((1, 2), F32),
            pltpu.VMEM((1, 2), F32),
            pltpu.VMEM((ys, BLOCKS, 2, 4, N), BF16),
            pltpu.VMEM((BLOCKS, ys, ws, 2, 4, N), BF16),
            pltpu.VMEM((ys, 4, ws * width), BF16),
            pltpu.VMEM((ys, ws, 4, width), BF16),
            pltpu.VMEM((length // BLOCKS, width), BF16),
            pltpu.VMEM((PAD + length, width), F32),
            pltpu.VMEM((length, width), F32),
            pltpu.VMEM((length, width), F32),
            pltpu.VMEM((length, width), F32),
            pltpu.VMEM((length, N), BF16),
            pltpu.VMEM((chunks, N, chunk), BF16),
            pltpu.VMEM((length, chunk), BF16),
            pltpu.VMEM((N, width), F32),
            pltpu.VMEM((length, width), BF16),
            pltpu.VMEM((length, width), BF16),
            pltpu.VMEM((length + PAD, width), F32),
            pltpu.VMEM((BLOCKS, ys, ws, 4, width), BF16),
            pltpu.VMEM((BLOCKS, ys, 4, ws * width), BF16),
            dma((5,)),
            dma((1,)),
            dma((BLOCKS,)),
            dma((1,)),
            dma((BLOCKS,)),
            dma((BLOCKS,)),
            dma((3,)),
            dma((1,)),
            dma((1,)),
            dma((1,)),
            dma((chunks,)),
            dma((1,)),
            dma((BLOCKS * halves,)),
            dma((1,)),
            dma((1,)),
            dma((2,)),
            pltpu.SemaphoreType.REGULAR((1,)),
        ],
        compiler_params=pltpu.CompilerParams(
            collective_id=0, has_side_effects=True, vmem_limit_bytes=40 * 1024 * 1024
        ),
    )(
        *(
            pltpu.with_memory_space_constraint(array, pltpu.HBM)
            for array in (
                activations[0],
                conv_weight[0],
                step_size[0].T,
                decay_rate,
                skip_gain,
                b_matrix[0],
                c_matrix[0],
                top_grad,
            )
        )
    )
    return (out[None], conv[None])


def solution(mesh):
    return jax.shard_map(
        on_device,
        mesh=mesh,
        in_specs=(
            P("section", None, "tensor"),
            P("section", None, "tensor"),
            P("section", None, "tensor"),
            P("section", "tensor"),
            P("section", "tensor"),
            P("section", None, "tensor", None),
            P("section", None, "tensor", None),
            P(None, "tensor", None),
        ),
        out_specs=(P("section", None, "tensor", None), P("section", None, "tensor")),
        check_vma=False,
    )
```

```python
import functools

import jax
import jax.numpy as jnp
from jax import lax
from jax.experimental import pallas as pl
from jax.experimental.pallas import tpu as pltpu
from jax.sharding import PartitionSpec as P

P_SIZE = 64
N = 256
K = 4
BLOCKS = 4
CHUNK = 64
HALVES = 2
EARLY = 3
LAG = 3
PACED = 6
ROUND = (12, 10, 8, 6, 4)
PAD = 8
F32 = jnp.float32
BF16 = jnp.bfloat16


def dot(a, b):
    return jnp.dot(a, b, preferred_element_type=F32)


def kernel(
    sizes,
    act_ref,
    taps_ref,
    step_ref,
    rate_ref,
    skip_ref,
    b_ref,
    c_ref,
    top_ref,
    out_ref,
    conv_ref,
    act_in,
    taps_in,
    step_in,
    rate_in,
    skip_in,
    bc_rows,
    bc_all,
    top_rows,
    top_all,
    top_block,
    act_pad,
    slope,
    grow,
    shrink,
    b_flat,
    c_turned,
    scores,
    carried,
    dy,
    stream,
    extended,
    passing,
    out_send,
    out_rows,
    in_sem,
    bc1_s,
    bc1_r,
    bc2_s,
    bc2_r,
    bc3_r,
    top_s,
    top1_r,
    top2_r,
    hop_s,
    hop_r,
    pass_s,
    pass_r,
    out1_s,
    out1_r,
    out2_s,
    out2_r,
    out3_s,
    ready,
):
    sections, ys, ws, chunk, halves = sizes
    block = 4 * ys * ws
    length = BLOCKS * block
    chunks = length // chunk
    per_block = block // chunk
    per_half = per_block // halves
    ysub = ys // halves
    zs = ws // 2
    width = 2 * P_SIZE
    wide = ws * width
    sec = lax.axis_index("section")
    pos = lax.axis_index("tensor")
    y = pos // ws
    w = pos % ws
    z = w // 2
    core = w % 2
    top = sections - 1
    crossing = sections // 2
    last_block = BLOCKS - 1
    downward = range(BLOCKS - 1, -1, -1)

    def remote(src, dst, send, recv, section, tensor):
        return pltpu.make_async_remote_copy(
            src_ref=src,
            dst_ref=dst,
            send_sem=send,
            recv_sem=recv,
            device_id=(section, tensor),
            device_id_type=pl.DeviceIdType.MESH,
        )

    def wait_bytes(like, sem):
        pltpu.make_async_copy(like, like, sem).wait()

    def columns(of, size):
        return pl.ds(pl.multiple_of(of * size, size), size)

    def to_y(d):
        return lax.rem(y + d, ys)

    def to_w(d):
        return lax.rem(w + d, ws)

    def at_y(d):
        return to_y(d) * ws + w

    def at_w(d):
        return y * ws + to_w(d)

    sibling = y * ws + z * 2 + (1 - core)
    below = lax.rem(sec + sections - 1, sections)

    fetches = [
        pltpu.make_async_copy(src, dst, in_sem.at[i])
        for i, (src, dst) in enumerate(
            (
                (act_ref, act_in),
                (taps_ref, taps_in),
                (step_ref, step_in),
                (rate_ref, rate_in),
                (skip_ref, skip_in),
            )
        )
    ]

    barrier = pltpu.get_barrier_semaphore()

    def greet(section, tensor):
        pl.semaphore_signal(
            barrier, inc=1, device_id=(section, tensor), device_id_type=pl.DeviceIdType.MESH
        )

    for d in range(1, ys):
        greet(sec, at_y(d))
    for d in range(1, ws):
        greet(sec, at_w(d))

    @pl.when(sec < top)
    def _():
        greet(sec + 1, pos)

    @pl.when(sec < BLOCKS)
    def _():
        greet(top, pos)

    for fetch in fetches:
        fetch.start()
    below_greets = jnp.where(sec > 0, 1, 0)
    helpers_greet = jnp.where(sec == top, BLOCKS, 0)
    pl.semaphore_wait(barrier, ys + ws - 2 + below_greets + helpers_greet)

    @pl.when(sec == top)
    def _():
        for to in range(BLOCKS):
            pl.semaphore_signal(
                ready.at[0], inc=1, device_id=(to, pos), device_id_type=pl.DeviceIdType.MESH
            )


    helper = sec < BLOCKS
    top_at = jnp.where(sec == 3, 0, jnp.where(sec == 2, 3, jnp.where(sec == 1, 1, 2)))

    def top1(d):
        return remote(
            top_ref.at[top_at, :, columns(to_y(d), wide)],
            top_rows.at[y],
            top_s.at[0],
            top1_r.at[0],
            sec,
            at_y(d),
        )

    def top2(d):
        return remote(
            top_rows.at[:, :, columns(to_w(d), width)],
            top_all.at[:, w],
            top_s.at[1],
            top2_r.at[0],
            sec,
            at_w(d),
        )

    def top3(part):
        return remote(
            top_block.at[pl.ds(part * chunk, chunk), :],
            dy.at[pl.ds(pl.multiple_of(top_at * block + part * chunk, chunk), chunk), :],
            top_s.at[2],
            hop_r.at[top_at * per_block + part],
            top,
            pos,
        )

    @pl.when(helper)
    def _():
        for d in range(1, ys):
            top1(d).start()
        pltpu.make_async_copy(
            top_ref.at[top_at, :, columns(y, wide)], top_rows.at[y], top1_r.at[0]
        ).start()

    def bc1(at, which, d):
        return remote(
            (b_ref, c_ref)[which].at[at, :, columns(to_y(d), N)],
            bc_rows.at[y, at, which],
            bc1_s.at[0],
            bc1_r.at[at],
            sec,
            at_y(d),
        )

    for at in downward:
        for d in range(1, ys):
            for which in range(2):
                bc1(at, which, d).start()
        for which in range(2):
            pltpu.make_async_copy(
                (b_ref, c_ref)[which].at[at, :, columns(y, N)],
                bc_rows.at[y, at, which],
                bc1_r.at[at],
            ).start()

    @pl.when(helper)
    def _():
        wait_bytes(top_rows, top1_r.at[0])
        for d in range(1, ws):
            top2(d).start()
        pltpu.make_async_copy(
            top_rows.at[:, :, columns(w, width)], top_all.at[:, w], top2_r.at[0]
        ).start()

    def bc2(at, d):
        to = sibling if d == 0 else y * ws + lax.rem(z + d, zs) * 2 + core
        recv = bc3_r if d == 0 else bc2_r
        return remote(bc_rows.at[:, at], bc_all.at[at, :, w], bc2_s.at[0], recv.at[at], sec, to)

    def bc3(at, d):
        piece = bc_all.at[at, :, lax.rem(z + zs - d, zs) * 2 + core]
        return remote(piece, piece, bc2_s.at[0], bc3_r.at[at], sec, sibling)

    def spread(at):
        for d in range(zs - 1, -1, -1):
            bc2(at, d).start()
        pltpu.make_async_copy(bc_rows.at[:, at], bc_all.at[at, :, w], bc3_r.at[at]).start()

    paced = sec >= PACED * sections // 8

    def collect(at):
        wait_bytes(bc_all.at[at, :, 0 : zs - 1], bc2_r.at[at])

        if at >= 2:

            @pl.when(paced)
            def _():
                spread(at - 2)

        for d in range(1, zs):
            bc3(at, d).start()

    wait_bytes(bc_rows.at[:, last_block], bc1_r.at[last_block])
    spread(last_block)

    for fetch in fetches:
        fetch.wait()
    act_pad[0:PAD, :] = jnp.zeros((PAD, width), F32)
    act_pad[PAD:, :] = act_in[...].astype(F32)
    taps = taps_in[...].astype(F32)
    first = lax.broadcasted_iota(jnp.int32, (1, width), 1) < P_SIZE
    rate = jnp.where(first, rate_in[:, 0:1], rate_in[:, 1:2])
    skip = jnp.where(first, skip_in[:, 0:1], skip_in[:, 1:2])
    row_at = lax.broadcasted_iota(jnp.int32, (chunk, chunk), 0)
    col_at = lax.broadcasted_iota(jnp.int32, (chunk, chunk), 1)
    lower = (row_at >= col_at).astype(F32).astype(BF16)
    for at in range(chunks):
        rows = slice(at * chunk, (at + 1) * chunk)
        preact = jnp.zeros((chunk, width), F32)
        for k in range(K):
            start = PAD + at * chunk - k
            preact = preact + taps[k : k + 1] * act_pad[start : start + chunk, :]
        logistic = 1.0 / (1.0 + jnp.exp(-preact))
        slope_here = logistic * (1.0 + preact * (1.0 - logistic))
        step = jnp.concatenate(
            [jnp.broadcast_to(step_in[h : h + 1, rows], (P_SIZE, chunk)) for h in range(2)], axis=0
        ).T
        high = step.astype(BF16)
        rest = step - high.astype(F32)
        mid = rest.astype(BF16)
        low = (rest - mid.astype(F32)).astype(BF16)
        decay = -rate * (dot(lower, high) + dot(lower, mid) + dot(lower, low))
        grow[rows, :] = jnp.exp(decay)
        shrink[rows, :] = step * jnp.exp(-decay) * slope_here
        slope[rows, :] = skip * slope_here
    carried[...] = jnp.zeros_like(carried)
    extended[length:, :] = jnp.zeros((PAD, width), F32)

    wait_bytes(bc_rows.at[:, last_block - 1], bc1_r.at[last_block - 1])
    spread(last_block - 1)
    for at in range(last_block - 2, -1, -1):
        wait_bytes(bc_rows.at[:, at], bc1_r.at[at])

    @pl.when(jnp.logical_not(paced))
    def _():
        for at in range(last_block - 2, -1, -1):
            spread(at)

    @pl.when(helper)
    def _():
        wait_bytes(top_all, top2_r.at[0])
        gathered = top_all[...].reshape(block, width)

        top_block[...] = gathered
        pl.semaphore_wait(ready.at[0], 1)
        for part in range(per_block - 1, -1, -1):
            top3(part).start()

    @pl.when(jnp.logical_not(paced))
    def _():
        for at in downward:
            collect(at)

    def hop(at):
        rows = pl.ds(at * chunk, chunk)
        return remote(
            stream.at[rows, :], dy.at[rows, :], hop_s.at[0], hop_r.at[at], below, pos
        )

    def round_out(at):
        slot = ROUND.index(at)
        return remote(
            stream.at[pl.ds(at * chunk, chunk), :],
            passing.at[slot],
            hop_s.at[0],
            pass_r.at[slot],
            top,
            pos,
        )

    def round_on(at):
        return remote(
            passing.at[ROUND.index(at)],
            dy.at[pl.ds(at * chunk, chunk), :],
            pass_s.at[0],
            hop_r.at[at],
            crossing - 1,
            pos,
        )

    def out1(at, half, d):
        group = pl.ds(half * ysub, ysub)
        return remote(
            out_send.at[at, group, to_w(d)],
            out_rows.at[at, group, :, columns(w, width)],
            out1_s.at[0],
            out1_r.at[at * halves + half],
            sec,
            at_w(d),
        )

    def out2(at, half, d):
        to = half * ysub + lax.rem(y + d, ysub)
        return remote(
            out_rows.at[at, to],
            out_ref.at[at, :, columns(y, wide)],
            out2_s.at[0],
            out2_r.at[0],
            sec,
            to * ws + w,
        )

    def out3(to, d):
        return remote(
            out_send.at[0, to, to_w(d)],
            out_ref.at[0, :, columns(pos, width)],
            out3_s.at[0 if d else 1],
            out2_r.at[0],
            sec,
            to * ws + to_w(d),
        )

    def send_last():
        out_send[0, 0:ysub] = stream[0 : block // halves, :].reshape(ysub, ws, 4, width)
        for to in range(ysub):
            for d in range(1, ws):
                out3(to, d).start()

            @pl.when(y == to)
            def _():
                pltpu.make_async_copy(
                    out_send.at[0, to, w], out_ref.at[0, :, columns(pos, width)], out2_r.at[0]
                ).start()

            @pl.when(y != to)
            def _():
                out3(to, 0).start()

    def start_rows(at, half):
        group = pl.ds(half * ysub, ysub)
        begin = at * block + half * (block // halves)
        out_send[at, half * ysub : (half + 1) * ysub] = stream[
            begin : begin + block // halves, :
        ].reshape(ysub, ws, 4, width)
        for d in range(1, ws):
            out1(at, half, d).start()
        pltpu.make_async_copy(
            out_send.at[at, group, w],
            out_rows.at[at, group, :, columns(w, width)],
            out1_r.at[at * halves + half],
        ).start()

    def forward_rows(at, half):
        wait_bytes(out_rows.at[at, pl.ds(half * ysub, ysub)], out1_r.at[at * halves + half])
        for d in range(1, ysub):
            out2(at, half, d).start()
        mine = y // ysub == half

        @pl.when(mine)
        def _():
            pltpu.make_async_copy(
                out_rows.at[at, y], out_ref.at[at, :, columns(y, wide)], out2_r.at[0]
            ).start()

        @pl.when(jnp.logical_not(mine))
        def _():
            out2(at, half, 0).start()

    units = [(at, half) for at in downward for half in range(halves - 1, -1, -1)]
    done = 0
    for at in downward:
        @pl.when(paced)
        def _():
            collect(at)

        wait_bytes(bc_all.at[at, :, 0 : zs + 1], bc3_r.at[at])
        start = at * block
        b_flat[start : start + block, :] = bc_all[at, :, :, 0].reshape(block, N)
        c_here = bc_all[at, :, :, 1].reshape(block, N)
        for part in range(per_block):
            inner = slice(part * chunk, (part + 1) * chunk)
            rows = slice(start + part * chunk, start + (part + 1) * chunk)
            product = lax.dot_general(
                b_flat[rows, :], c_here[inner], (((1,), (1,)), ((), ())), preferred_element_type=F32
            )
            scores[rows, :] = jnp.where(col_at >= row_at, product, 0.0).astype(BF16)
            c_turned[at * per_block + part] = c_here[inner].T

        for part in range(per_block - 1, -1, -1):
            here = at * per_block + part
            rows = slice(here * chunk, (here + 1) * chunk)
            ended = grow[(here + 1) * chunk - 1 : (here + 1) * chunk, :] * carried[...]
            through = dot(b_flat[rows, :], ended.astype(BF16))

            hop(here).wait_recv()
            upstream = dy[rows, :].astype(F32)
            fed = (grow[rows, :] * upstream).astype(BF16)
            mixed = dot(scores[rows, :], fed) + through
            update = dot(c_turned[here], fed)
            grad_pre = shrink[rows, :] * mixed + slope[rows, :] * upstream
            extended[rows, :] = grad_pre
            grad_in = taps[0:1] * grad_pre
            for k in range(1, K):
                begin = here * chunk + k
                grad_in = grad_in + taps[k : k + 1] * extended[begin : begin + chunk, :]
            stream[rows, :] = (upstream + grad_in.astype(BF16).astype(F32)).astype(BF16)

            if here in ROUND:

                @pl.when((sec > 0) & (sec != crossing))
                def _():
                    hop(here).start()

                @pl.when(sec == crossing)
                def _():
                    round_out(here).start()

            else:

                @pl.when(sec > 0)
                def _():
                    hop(here).start()

            if here > 0:
                carried[...] = ended + update
            if part % per_half == 0:
                done += 1

                @pl.when(sec < EARLY)
                def _():
                    if done < len(units):
                        start_rows(*units[done - 1])
                    else:
                        send_last()
                    if done > LAG:
                        forward_rows(*units[done - 1 - LAG])

    @pl.when(sec == top)
    def _():
        for slot, at in enumerate(ROUND):
            wait_bytes(passing.at[slot], pass_r.at[slot])
            round_on(at).start()

    @pl.when(sec >= EARLY)
    def _():
        for unit in units[:-1]:
            start_rows(*unit)
        send_last()
        for unit in units[:-LAG]:
            forward_rows(*unit)

    for unit in units[-LAG:-1]:
        forward_rows(*unit)

    conv = [jnp.zeros((1, width), F32) for _ in range(K)]
    for at in range(chunks):
        for k in range(K):
            start = PAD + at * chunk - k
            conv[k] = conv[k] + jnp.sum(
                extended[at * chunk : (at + 1) * chunk, :] * act_pad[start : start + chunk, :],
                axis=0,
                keepdims=True,
            )
    for k in range(K):
        conv_ref[k : k + 1, :] = conv[k]

    wait_bytes(bc_rows.at[0 : ys - 1], bc1_s.at[0])
    wait_bytes(bc_all.at[:, :, 0 : 2 * zs - 1], bc2_s.at[0])

    @pl.when(helper)
    def _():
        wait_bytes(top_rows.at[0 : ys - 1], top_s.at[0])
        wait_bytes(top_all.at[:, 0 : ws - 1], top_s.at[1])
        wait_bytes(top_block, top_s.at[2])

    @pl.when(sec == top)
    def _():
        wait_bytes(passing, pass_s.at[0])

    @pl.when(sec > 0)
    def _():
        wait_bytes(stream, hop_s.at[0])

    wait_bytes(out_send.at[1:BLOCKS, :, 0 : ws - 1], out1_s.at[0])
    wait_bytes(out_send.at[0, ysub:ys, 0 : ws - 1], out1_s.at[0])
    for at in range(1, BLOCKS):
        wait_bytes(out_rows.at[at, 0 : ys - 1], out2_s.at[0])
    wait_bytes(out_send.at[0, 0:ysub, 0 : ws - 1], out3_s.at[0])
    in_last = y // ysub == 0

    @pl.when(in_last)
    def _():
        wait_bytes(out_rows.at[0, 0 : ys - ysub], out2_s.at[0])
        wait_bytes(out_send.at[0, 0 : ysub - 1, 0], out3_s.at[1])

    @pl.when(jnp.logical_not(in_last))
    def _():
        wait_bytes(out_rows.at[0, 0 : ys - ysub - 1], out2_s.at[0])
        wait_bytes(out_send.at[0, 0:ysub, 0], out3_s.at[1])

    wait_bytes(out_ref, out2_r.at[0])


def on_device(
    activations, conv_weight, step_size, decay_rate, skip_gain, b_matrix, c_matrix, top_grad
):
    tensor_size = lax.axis_size("tensor")
    sections = lax.axis_size("section")
    ys = b_matrix.shape[-1] // N
    ws = tensor_size // ys
    length, width = activations.shape[1:]
    chunk = min(CHUNK, length // BLOCKS)
    chunks = length // chunk
    halves = min(HALVES, length // BLOCKS // chunk)
    dma = pltpu.SemaphoreType.DMA
    out, conv = pl.pallas_call(
        functools.partial(kernel, (sections, ys, ws, chunk, halves)),
        out_shape=(
            jax.ShapeDtypeStruct(top_grad.shape, BF16),
            jax.ShapeDtypeStruct((K, width), F32),
        ),
        in_specs=[pl.BlockSpec(memory_space=pltpu.HBM)] * 8,
        out_specs=(pl.BlockSpec(memory_space=pltpu.VMEM),) * 2,
        scratch_shapes=[
            pltpu.VMEM((length, width), BF16),
            pltpu.VMEM((K, width), BF16),
            pltpu.VMEM((2, length), F32),
            pltpu.VMEM((1, 2), F32),
            pltpu.VMEM((1, 2), F32),
            pltpu.VMEM((ys, BLOCKS, 2, 4, N), BF16),
            pltpu.VMEM((BLOCKS, ys, ws, 2, 4, N), BF16),
            pltpu.VMEM((ys, 4, ws * width), BF16),
            pltpu.VMEM((ys, ws, 4, width), BF16),
            pltpu.VMEM((length // BLOCKS, width), BF16),
            pltpu.VMEM((PAD + length, width), F32),
            pltpu.VMEM((length, width), F32),
            pltpu.VMEM((length, width), F32),
            pltpu.VMEM((length, width), F32),
            pltpu.VMEM((length, N), BF16),
            pltpu.VMEM((chunks, N, chunk), BF16),
            pltpu.VMEM((length, chunk), BF16),
            pltpu.VMEM((N, width), F32),
            pltpu.VMEM((length, width), BF16),
            pltpu.VMEM((length, width), BF16),
            pltpu.VMEM((length + PAD, width), F32),
            pltpu.VMEM((len(ROUND), chunk, width), BF16),
            pltpu.VMEM((BLOCKS, ys, ws, 4, width), BF16),
            pltpu.VMEM((BLOCKS, ys, 4, ws * width), BF16),
            dma((5,)),
            dma((1,)),
            dma((BLOCKS,)),
            dma((1,)),
            dma((BLOCKS,)),
            dma((BLOCKS,)),
            dma((3,)),
            dma((1,)),
            dma((1,)),
            dma((1,)),
            dma((chunks,)),
            dma((1,)),
            dma((len(ROUND),)),
            dma((1,)),
            dma((BLOCKS * halves,)),
            dma((1,)),
            dma((1,)),
            dma((2,)),
            pltpu.SemaphoreType.REGULAR((1,)),
        ],
        compiler_params=pltpu.CompilerParams(
            collective_id=0, has_side_effects=True, vmem_limit_bytes=40 * 1024 * 1024
        ),
    )(
        *(
            pltpu.with_memory_space_constraint(array, pltpu.HBM)
            for array in (
                activations[0],
                conv_weight[0],
                step_size[0].T,
                decay_rate,
                skip_gain,
                b_matrix[0],
                c_matrix[0],
                top_grad,
            )
        )
    )
    return (out[None], conv[None])


def solution(mesh):
    return jax.shard_map(
        on_device,
        mesh=mesh,
        in_specs=(
            P("section", None, "tensor"),
            P("section", None, "tensor"),
            P("section", None, "tensor"),
            P("section", "tensor"),
            P("section", "tensor"),
            P("section", None, "tensor", None),
            P("section", None, "tensor", None),
            P(None, "tensor", None),
        ),
        out_specs=(P("section", None, "tensor", None), P("section", None, "tensor")),
        check_vma=False,
    )
```
